32 devices in a mesh: depth: 2 (over y), row: 4 (over x, core), col: 4 (over z).
Axes of the slice: x: 2, y: 2, z: 4, core: 2. Of those that a mesh axis runs over, the one named last changes fastest.
Arguments:
- state: float32 [4, 32, 64, 512], P(None, 'depth', 'row', 'col'), may hold values from 0 to 1
- velocity: float32 [3, 32, 64, 512], P(None, 'depth', 'row', 'col'), may hold values from -3 to 3
- view_order: int32 [4, 4], P('row', 'col'), may hold values from 0 to 1
- tf_table: int32 [4, 256], replicated, may hold values from 0 to 255
Outputs:
- new_state: float32 [4, 32, 64, 512], P(None, 'depth', 'row', 'col')
- image: float32 [4, 256, 256], P(None, 'row', 'col')
The draws below stay inside these ranges and needn't reach their ends.
Inputs may be any that keep to these rules, and one draw needn't show every extreme that they name: `view_order`: 0 puts the lowest depth indices in front, 1 the highest. `tf_table`: levels in units of 1/255.
All inputs are finite; a program needn't handle non-finite values.
Results may differ from the reference program's by a relative error of at most 0.0003.
Values sent between devices are 32-bit elements; how exact they have to be, the bound alone decides.
No kernel may reach another device: no remote copies, remote signals or barrier semaphores. Data moves between devices by JAX's collectives and lax.ppermute only.
A program may use at most 128 MiB of HBM per device.

```python
import jax
import jax.numpy as jnp
from jax import lax

CR = 16
CC = 128
PIX_R = 64
PIX_C = 64
BINS = 256
ND = 32
NR = 64
NC = 512
HEIGHT = 256
WIDTH = 256
N_ROW = 4
N_COL = 4


def draw_state(key, part):
    shape = (4, ND, NR, NC)
    first_key = jax.random.fold_in(key, 11)
    second_key = jax.random.fold_in(key, 12)
    chooser = jax.random.uniform(first_key, shape, jnp.float32)
    jitter = jax.random.uniform(second_key, shape, jnp.float32)
    spread = 0.15
    values = jnp.where(chooser >= 0.5, 1.0 - spread * jitter, spread * jitter)
    return jnp.clip(values, 0.0, 1.0).astype(jnp.float32)


def draw_velocity(key, part):
    shape = (3, ND, NR, NC)
    first_key = jax.random.fold_in(key, 21)
    second_key = jax.random.fold_in(key, 22)
    chooser = jax.random.uniform(first_key, shape, jnp.float32)
    magnitude = jax.random.uniform(second_key, shape, jnp.float32, 2.0, 3.0)
    signed = jnp.where(chooser >= 0.5, magnitude, -magnitude)
    return jnp.clip(signed, -3.0, 3.0).astype(jnp.float32)


def with_ends(values, stream_key, smallest, high):
    shape = values.shape
    index_at = [jax.random.randint(jax.random.fold_in(stream_key, axis), (), 0, shape[axis]) for axis in range(len(shape))]
    values = values.at[tuple(index_at)].set(smallest)
    longest = shape.index(max(shape))
    index_at[longest] = (index_at[longest] + 1) % shape[longest]
    return values.at[tuple(index_at)].set(high)


def setup_inputs(seed: int = 0) -> dict:
    key_of = jax.random.split(jax.random.key(seed), 5)
    return {
        "state": draw_state(jax.random.fold_in(key_of[4], 71), 0),
        "velocity": draw_velocity(jax.random.fold_in(key_of[4], 71), 0),
        "view_order": with_ends(jax.random.randint(key_of[2], (N_ROW, N_COL), 0, 2), jax.random.fold_in(key_of[2], 1), 0, 1).astype(jnp.int32),
        "tf_table": with_ends(jax.random.randint(key_of[3], (4, BINS), 0, 256), jax.random.fold_in(key_of[3], 1), 0, 255).astype(jnp.int32),
    }


FIRST_COEF = (0.8, -0.2, 4.0 / 105.0, -1.0 / 280.0)
SECOND_COEF = (1.6, -0.2, 8.0 / 315.0, -1.0 / 560.0)
CENTER_COEF = -205.0 / 72.0
DIFFUSIVITY = (0.05, 0.04, 0.03, 0.08)
TIME_STEP = 0.2
RATE_CONST = 2.0
IGNITION_SLOPE = 8.0
IGNITION_TEMP = 0.5
OXIDIZER_RATIO = 1.5
HEAT_RELEASE = 0.8
SHEAR_CELLS = 2.0
OPACITY_TOTAL = 6.0


def source_terms(centre):
    rate = RATE_CONST * centre[0] * centre[1] * jax.nn.sigmoid(IGNITION_SLOPE * (centre[3] - IGNITION_TEMP))
    return jnp.stack([-rate, -OXIDIZER_RATIO * rate, (1.0 + OXIDIZER_RATIO) * rate, HEAT_RELEASE * rate])


def combine_terms(centre, gradients, laplace, velocity):
    advect = velocity[0][None] * gradients[0] + velocity[1][None] * gradients[1] + velocity[2][None] * gradients[2]
    diffusion = jnp.stack([DIFFUSIVITY[field_index] * laplace[field_index] for field_index in range(4)])
    return diffusion - advect + source_terms(centre)


def tendency(state, velocity):
    laplace = (3.0 * CENTER_COEF) * state
    gradients = []
    for spatial in (1, 2, 3):
        gradient = jnp.zeros_like(state)
        for offset in range(4):
            forward = jnp.roll(state, -(offset + 1), spatial)
            backward = jnp.roll(state, offset + 1, spatial)
            gradient = gradient + FIRST_COEF[offset] * (forward - backward)
            laplace = laplace + SECOND_COEF[offset] * (forward + backward)
        gradients.append(gradient)
    return combine_terms(state, gradients, laplace, velocity)


def row_matrix(slice_total, cell_count, pixels):
    stride = cell_count / pixels
    spread = max(1.0, stride)
    centres = (jnp.arange(pixels, dtype=jnp.float32) + 0.5) * stride - 0.5
    shifts = SHEAR_CELLS * ((jnp.arange(slice_total, dtype=jnp.float32) + 0.5) / slice_total - 0.5)
    places = jnp.clip(centres[None, :] + shifts[:, None], 0.0, cell_count - 1.0)
    cells_at = jnp.arange(cell_count, dtype=jnp.float32)
    return jnp.maximum(0.0, 1.0 - jnp.abs(places[:, :, None] - cells_at[None, None, :]) / spread) / spread


def column_matrix(cell_count, pixels):
    stride = cell_count / pixels
    spread = max(1.0, stride)
    centres = jnp.clip((jnp.arange(pixels, dtype=jnp.float32) + 0.5) * stride - 0.5, 0.0, cell_count - 1.0)
    cells_at = jnp.arange(cell_count, dtype=jnp.float32)
    return jnp.maximum(0.0, 1.0 - jnp.abs(centres[None, :] - cells_at[:, None]) / spread) / spread


def shade_lookup(values, table_values, slice_total):
    levels = table_values.shape[1]
    level = jnp.clip(values, 0.0, 1.0) * (levels - 1.0)
    lower = jnp.clip(jnp.floor(level), 0.0, levels - 2.0)
    fraction = level - lower
    index = lower.astype(jnp.int32)
    below = jnp.take(table_values, index, axis=1)
    above = jnp.take(table_values, index + 1, axis=1)
    raw_colour = (below * (1.0 - fraction)[None, :] + above * fraction[None, :]) * (1.0 / 255.0)
    opacity = (OPACITY_TOTAL / slice_total) * raw_colour[3]
    return jnp.concatenate([opacity[None, :] * raw_colour[:3], opacity[None, :]], 0)


def march_ordered(sampled, table_values, slice_total):
    def advance(running, values):
        accumulated, transmit = running
        colour = shade_lookup(values, table_values, slice_total)
        return (accumulated + transmit[None, :] * colour, transmit * (1.0 - colour[3])), None

    start = (jnp.zeros((4, sampled.shape[1]), jnp.float32), jnp.ones((sampled.shape[1],), jnp.float32))
    finished, unused = lax.scan(advance, start, sampled)
    return finished[0]


def reference(state, velocity, view_order, tf_table):
    first_rate = tendency(state, velocity)
    middle = state + TIME_STEP * first_rate
    second_rate = tendency(middle, velocity)
    new_state = state + (0.5 * TIME_STEP) * (first_rate + second_rate)
    temper = new_state[3].reshape(ND, N_ROW, CR, N_COL, CC)
    row_weights = row_matrix(ND, CR, PIX_R)
    column_weights = column_matrix(CC, PIX_C)
    partial_rows = jnp.einsum("dpr,dirjc->dipjc", row_weights, temper, precision=lax.Precision.HIGHEST)
    sampled = jnp.einsum("dipjc,cq->dipjq", partial_rows, column_weights, precision=lax.Precision.HIGHEST)
    sampled = sampled.reshape(ND, HEIGHT * WIDTH)
    order_map = jnp.broadcast_to(view_order[:, None, :, None], (N_ROW, PIX_R, N_COL, PIX_C)).reshape(HEIGHT * WIDTH)
    ordered = jnp.where(order_map[None, :] == 0, sampled, sampled[::-1])
    table_values = tf_table.astype(jnp.float32)
    image = march_ordered(ordered, table_values, ND)
    return new_state, image.reshape(4, HEIGHT, WIDTH)
```

```python
import functools

import jax
import jax.numpy as jnp
import numpy as np
from jax import lax
from jax.experimental import pallas as pl
from jax.experimental.pallas import tpu as pltpu
from jax.sharding import PartitionSpec as P

PIX_R = 64
PIX_C = 64
HALO = 4

FIRST_COEF = (0.8, -0.2, 4.0 / 105.0, -1.0 / 280.0)
SECOND_COEF = (1.6, -0.2, 8.0 / 315.0, -1.0 / 560.0)
CENTER_COEF = -205.0 / 72.0
FIRST_SCALE = 840
SECOND_SCALE = 5040
DIFFUSIVITY = (0.05, 0.04, 0.03, 0.08)
TIME_STEP = 0.2
RATE_CONST = 2.0
IGNITION_SLOPE = 8.0
IGNITION_TEMP = 0.5
OXIDIZER_RATIO = 1.5
HEAT_RELEASE = 0.8
SHEAR_CELLS = 2.0
OPACITY_TOTAL = 6.0
SOURCE_COEF = (-1.0, -OXIDIZER_RATIO, 1.0 + OXIDIZER_RATIO, HEAT_RELEASE)

VMEM_LIMIT = 24 * 1024 * 1024
F32 = jnp.float32
BF16 = jnp.bfloat16


def column_stencil(columns):
    band = np.zeros((columns + 2 * HALO, 2 * columns), np.float32)
    for column in range(columns):
        for k in range(HALO):
            first = round(FIRST_COEF[k] * FIRST_SCALE)
            second = round(SECOND_COEF[k] * SECOND_SCALE)
            ahead, behind = column + HALO + k + 1, column + HALO - k - 1
            band[ahead, column] += first
            band[behind, column] -= first
            band[ahead, columns + column] += second
            band[behind, columns + column] += second
    inner = band[HALO : HALO + columns]
    halo = np.concatenate([band[:HALO], band[HALO + columns :]], 0)
    return inner, halo


def stencil_weights(columns):
    inner, halo = column_stencil(columns)
    spread = np.tile(halo, (columns // (2 * HALO), 1))
    return np.concatenate([inner, inner], 0), np.concatenate([spread, spread], 0)


def column_matrix(cell_count, pixels):
    stride = cell_count / pixels
    spread = max(1.0, stride)
    centres = np.clip((np.arange(pixels) + 0.5) * stride - 0.5, 0.0, cell_count - 1.0)
    cells_at = np.arange(cell_count)
    return np.maximum(0.0, 1.0 - np.abs(centres[None, :] - cells_at[:, None]) / spread) / spread


def halves(value):
    upper = value.astype(BF16)
    return upper, (value - upper.astype(F32)).astype(BF16)


def by_field(field, values):
    result = jnp.float32(values[-1])
    for index in range(len(values) - 2, -1, -1):
        result = jnp.where(field == index, jnp.float32(values[index]), result)
    return result


def pack_field(source, field, depth_out, low_out, high_out, column_out):
    _, depth, rows, columns = source.shape
    half = depth // 2
    depth_out[field, 0:HALO] = source[field, depth - HALO : depth]
    depth_out[field, HALO : 2 * HALO] = source[field, 0:HALO]
    for d in range(half):
        low_out[field, d, 0:HALO] = source[field, d, 0:HALO]
        low_out[field, d, HALO : 2 * HALO] = source[field, d + half, 0:HALO]
        high_out[field, d, 0:HALO] = source[field, d, rows - HALO : rows]
        high_out[field, d, HALO : 2 * HALO] = source[field, d + half, rows - HALO : rows]
    lane = lax.broadcasted_iota(jnp.int32, (rows, columns), 1)
    packed = jnp.zeros((rows, columns), F32)
    for d in range(depth):
        turned = pltpu.roll(source[field, d], (2 * HALO * d + HALO) % columns, 1)
        packed = jnp.where(lane // (2 * HALO) == d, turned, packed)
    column_out[field] = packed


def pack_kernel(state, depth_out, low_out, high_out, column_out):
    def each(field, carry):
        pack_field(state, field, depth_out, low_out, high_out, column_out)
        return carry

    lax.fori_loop(0, state.shape[0], each, 0)


def reaction(fields, rate):
    rate[...] = (
        RATE_CONST
        * fields[0]
        * fields[1]
        / (1.0 + jnp.exp(-IGNITION_SLOPE * (fields[3] - IGNITION_TEMP)))
    )


def field_tendency(
    fields, field, velocity, halos, weights, rate, padded, across, write
):
    depth_halo, row_below, row_above, column_below, column_above = halos
    inner_weight, halo_weight = weights
    _, depth, rows, columns = fields.shape
    half = depth // 2
    start = 2 * HALO

    flat = fields[field].reshape(depth * rows, columns)
    upper, lower = halves(flat)
    total = jnp.dot(
        jnp.concatenate([upper, lower], 1), inner_weight[...], preferred_element_type=F32
    )
    lane = lax.broadcasted_iota(jnp.int32, (rows, columns), 1)
    edge = jnp.where(lane % (2 * HALO) < HALO, column_below[field], column_above[field])
    edge_upper, edge_lower = halves(edge)
    spread = []
    for d in range(depth):
        own = lane // (2 * HALO) == d
        zero = jnp.zeros((rows, columns), BF16)
        spread.append(
            jnp.concatenate(
                [jnp.where(own, edge_upper, zero), jnp.where(own, edge_lower, zero)], 1
            )
        )
    total = total + jnp.dot(
        jnp.concatenate(spread, 0), halo_weight[...], preferred_element_type=F32
    )
    across[...] = total

    for d in range(depth):
        padded[d, start : start + rows] = fields[field, d]
        part = slice(0, HALO) if d < half else slice(HALO, 2 * HALO)
        padded[d, start - HALO : start] = row_below[field, d % half, part]
        padded[d, start + rows : start + rows + HALO] = row_above[field, d % half, part]

    def layer(d):
        if d < 0:
            return depth_halo[field, d + HALO]
        if d >= depth:
            return depth_halo[field, d - depth + HALO]
        return fields[field, d]

    diffusivity = by_field(field, DIFFUSIVITY)
    source = by_field(field, SOURCE_COEF)
    for d in range(depth):
        centre = fields[field, d]
        laplace = 3.0 * CENTER_COEF * centre
        along_depth = jnp.zeros_like(centre)
        along_row = jnp.zeros_like(centre)
        for k in range(HALO):
            ahead, behind = layer(d + k + 1), layer(d - k - 1)
            up = padded[d, start + k + 1 : start + k + 1 + rows]
            down = padded[d, start - k - 1 : start - k - 1 + rows]
            along_depth = along_depth + FIRST_COEF[k] * (ahead - behind)
            along_row = along_row + FIRST_COEF[k] * (up - down)
            laplace = laplace + SECOND_COEF[k] * ((ahead + behind) + (up + down))
        here = pl.ds(d * rows, rows)
        along_column = across[here, 0:columns] * (1.0 / FIRST_SCALE)
        laplace = laplace + across[here, columns : 2 * columns] * (1.0 / SECOND_SCALE)
        advect = (
            velocity[0, d] * along_depth
            + velocity[1, d] * along_row
            + velocity[2, d] * along_column
        )
        write(d, diffusivity * laplace - advect + source * rate[d])


def first_kernel(
    state,
    velocity,
    depth_halo,
    row_below,
    row_above,
    column_below,
    column_above,
    inner_weight,
    halo_weight,
    middle,
    depth_out,
    low_out,
    high_out,
    column_out,
    rate,
    padded,
    across,
):
    reaction(state, rate)
    halos = (depth_halo, row_below, row_above, column_below, column_above)

    def each(field, carry):
        def write(d, value):
            middle[field, d] = state[field, d] + TIME_STEP * value

        field_tendency(
            state, field, velocity, halos, (inner_weight, halo_weight), rate, padded, across, write
        )
        pack_field(middle, field, depth_out, low_out, high_out, column_out)
        return carry

    lax.fori_loop(0, state.shape[0], each, 0)


def sample_slices(temperature, column_weight, first_slice, slice_total, samples):
    depth, rows, columns = temperature.shape
    half = depth // 2
    upper, lower = halves(temperature[...].reshape(depth * rows, columns))
    wide = jnp.dot(
        jnp.concatenate([upper, lower], 1), column_weight[...], preferred_element_type=F32
    )
    lane = lax.broadcasted_iota(jnp.int32, (rows, 2 * PIX_C), 1)
    stride = rows / PIX_R
    reach = max(1.0, stride)
    shape = (PIX_R, 4 * rows)
    pixel = lax.broadcasted_iota(jnp.int32, shape, 0).astype(F32)
    place = lax.broadcasted_iota(jnp.int32, shape, 1)
    cell = (place % rows).astype(F32)
    later = (place // rows % 2) * half
    for i in range(half):
        level = (first_slice + i + later).astype(F32)
        shift = SHEAR_CELLS * ((level + 0.5) / slice_total - 0.5)
        at = jnp.clip((pixel + 0.5) * stride - 0.5 + shift, 0.0, rows - 1.0)
        weight = jnp.maximum(0.0, 1.0 - jnp.abs(at - cell) / reach) / reach
        left = jnp.where(lane < PIX_C, wide[i * rows : (i + 1) * rows], 0.0)
        right = jnp.where(
            lane < PIX_C, 0.0, wide[(i + half) * rows : (i + half + 1) * rows]
        )
        both = jnp.concatenate([left, right], 0)
        both_upper, both_lower = halves(both)
        samples[i] = jnp.dot(
            weight.astype(BF16),
            jnp.concatenate([both_upper, both_lower], 0),
            preferred_element_type=F32,
        )


def look_up(tables, index, shape):
    lanes = tables[0].shape[1]
    inside = index % lanes
    result = None
    for part, table in enumerate(tables):
        found = jnp.take_along_axis(
            jnp.broadcast_to(table, shape), inside, axis=1, mode="promise_in_bounds"
        )
        result = found if part == 0 else jnp.where(index >= part * lanes, found, result)
    return result


def march(samples, table, flag, slice_total, share):
    half, pixel_rows, lanes = samples.shape
    levels = table.shape[1]
    packed = table[0:1] + table[1:2] * 256 + table[2:3] * 65536 + table[3:4] * 16777216
    following = jnp.concatenate([packed[:, 1:], packed[:, levels - 1 :]], 1)
    below_tables = [packed[:, i : i + lanes] for i in range(0, levels, lanes)]
    above_tables = [following[:, i : i + lanes] for i in range(0, levels, lanes)]
    shape = (pixel_rows // 2, lanes)
    lane = lax.broadcasted_iota(jnp.int32, shape, 1)
    in_front = (lane < PIX_C) == (flag == 0)
    parts = []
    for part in range(2):
        rows_here = pl.ds(part * shape[0], shape[0])

        def advance(position, running):
            chosen = jnp.where(flag == 0, half - 1 - position, position)
            values = samples[chosen, rows_here]
            level = jnp.clip(values, 0.0, 1.0) * (levels - 1.0)
            lower = jnp.minimum(level.astype(jnp.int32), levels - 2)
            fraction = level - lower.astype(F32)
            below = look_up(below_tables, lower, shape)
            above = look_up(above_tables, lower, shape)
            raw = []
            for channel in range(4):
                low = (lax.shift_right_logical(below, 8 * channel) & 255).astype(F32)
                high = (lax.shift_right_logical(above, 8 * channel) & 255).astype(F32)
                raw.append(low + fraction * (high - low))
            alpha = raw[3] * (OPACITY_TOTAL / slice_total / 255.0)
            scaled = alpha * (1.0 / 255.0)
            through = 1.0 - alpha
            return tuple(
                [scaled * raw[c] + through * running[c] for c in range(3)]
                + [alpha + through * running[3]]
            )

        zero = jnp.zeros(shape, F32)
        parts.append(lax.fori_loop(0, half, advance, (zero, zero, zero, zero)))
    for channel in range(4):
        merged = []
        for part in range(2):
            own, own_alpha = parts[part][channel], parts[part][3]
            other, other_alpha = pltpu.roll(own, PIX_C, 1), pltpu.roll(own_alpha, PIX_C, 1)
            merged.append(
                jnp.where(
                    in_front, own + (1.0 - own_alpha) * other, other + (1.0 - other_alpha) * own
                )
            )
        share[channel] = jnp.where(lane < PIX_C, merged[0], merged[1])


def second_kernel(
    slice_total,
    order,
    place,
    middle,
    state,
    velocity,
    depth_halo,
    row_below,
    row_above,
    column_below,
    column_above,
    inner_weight,
    halo_weight,
    column_weight,
    table,
    new_state,
    share,
    rate,
    padded,
    across,
    samples,
):
    reaction(middle, rate)
    halos = (depth_halo, row_below, row_above, column_below, column_above)

    def each(field, carry):
        def write(d, value):
            new_state[field, d] = 0.5 * (state[field, d] + middle[field, d]) + (
                0.5 * TIME_STEP
            ) * value

        field_tendency(
            middle, field, velocity, halos, (inner_weight, halo_weight), rate, padded, across, write
        )
        return carry

    lax.fori_loop(0, state.shape[0], each, 0)
    depth = state.shape[1]
    sample_slices(new_state.at[3], column_weight, place[0] * depth, slice_total, samples)
    march(samples, table, order[0, 0], slice_total, share)


def merge_kernel(last, order, bit, own, received, out):
    front = order[0, 0] == bit[0]
    shape = own.shape[1:]
    own_alpha, received_alpha = own[3], received[3]
    for channel in range(4):
        one, two = own[channel], received[channel]
        front_value = one + (1.0 - own_alpha) * two
        back_value = two + (1.0 - received_alpha) * one
        value = jnp.where(front, front_value, back_value)
        if last:
            out[channel, 0 : shape[0]] = value[:, 0:PIX_C]
            out[channel, shape[0] : 2 * shape[0]] = pltpu.roll(value, PIX_C, 1)[:, 0:PIX_C]
        else:
            out[channel] = value


def shift(value, axis, step):
    count = lax.axis_size(axis)
    return lax.ppermute(value, axis, [(i, (i + step) % count) for i in range(count)])


def exchange(depth_faces, low_rows, high_rows, columns):
    if lax.axis_size("depth") == 2:
        depth_halo = shift(depth_faces, "depth", 1)
    else:
        depth_halo = jnp.concatenate(
            [
                shift(depth_faces[:, :HALO], "depth", 1),
                shift(depth_faces[:, HALO:], "depth", -1),
            ],
            1,
        )
    row_below = shift(high_rows, "row", 1)
    row_above = shift(low_rows, "row", -1)
    column_below = shift(columns, "col", 1)
    column_above = shift(columns, "col", -1)
    return depth_halo, row_below, row_above, column_below, column_above


def call(kernel, outs, scratch, specs, *args):
    vmem = pl.BlockSpec(memory_space=pltpu.VMEM)
    return pl.pallas_call(
        kernel,
        out_shape=outs,
        in_specs=specs + [vmem] * (len(args) - len(specs)),
        out_specs=jax.tree.map(lambda _: vmem, outs),
        scratch_shapes=scratch,
        compiler_params=pltpu.CompilerParams(vmem_limit_bytes=VMEM_LIMIT),
    )(*args)


def local(state, velocity, view_order, tf_table):
    fields, depth, rows, columns = state.shape
    depth_count = lax.axis_size("depth")
    smem = pl.BlockSpec(memory_space=pltpu.SMEM)

    def array(*shape):
        return jax.ShapeDtypeStruct(shape, F32)

    faces = (
        array(fields, 2 * HALO, rows, columns),
        array(fields, depth // 2, 2 * HALO, columns),
        array(fields, depth // 2, 2 * HALO, columns),
        array(fields, rows, columns),
    )
    inner, halo = stencil_weights(columns)
    inner_weight, halo_weight = jnp.asarray(inner, BF16), jnp.asarray(halo, BF16)
    narrow = column_matrix(columns, PIX_C)
    column_weight = jnp.asarray(np.tile(narrow, (2, 2)), BF16)
    work = [
        pltpu.VMEM((depth, rows, columns), F32),
        pltpu.VMEM((depth, rows + 4 * HALO, columns), F32),
        pltpu.VMEM((depth * rows, 2 * columns), F32),
    ]

    halos = exchange(*call(pack_kernel, faces, [], [], state))
    middle, *middle_faces = call(
        first_kernel,
        (array(*state.shape),) + faces,
        work,
        [],
        state,
        velocity,
        *halos,
        inner_weight,
        halo_weight,
    )
    halos = exchange(*middle_faces)
    depth_index = lax.axis_index("depth")
    new_state, share = call(
        functools.partial(second_kernel, depth * depth_count),
        (array(*state.shape), array(4, PIX_R // 2, 2 * PIX_C)),
        work + [pltpu.VMEM((depth // 2, PIX_R, 2 * PIX_C), F32)],
        [smem, smem],
        view_order,
        depth_index.reshape(1),
        middle,
        state,
        velocity,
        *halos,
        inner_weight,
        halo_weight,
        column_weight,
        tf_table,
    )
    bits = depth_count.bit_length() - 1
    for bit in range(bits):
        pairs = [(i, i ^ 2**bit) for i in range(depth_count)]
        received = lax.ppermute(share, "depth", pairs)
        last = bit == bits - 1
        share = call(
            functools.partial(merge_kernel, last),
            array(4, PIX_R, PIX_C) if last else array(*share.shape),
            [],
            [smem, smem],
            view_order,
            (depth_index // 2**bit % 2).reshape(1),
            share,
            received,
        )
    return new_state, share


def solution(mesh):
    in_specs = (
        P(None, "depth", "row", "col"),
        P(None, "depth", "row", "col"),
        P("row", "col"),
        P(),
    )
    out_specs = (P(None, "depth", "row", "col"), P(None, "row", "col"))
    return jax.shard_map(local, mesh=mesh, in_specs=in_specs, out_specs=out_specs, check_vma=False)
```

```python
import functools

import jax
import jax.numpy as jnp
from jax import lax
from jax.experimental import pallas as pl
from jax.experimental.pallas import tpu as pltpu
from jax.sharding import PartitionSpec as P

PIX_R = 64
PIX_C = 64
HALO = 4

FIRST_COEF = (0.8, -0.2, 4.0 / 105.0, -1.0 / 280.0)
SECOND_COEF = (1.6, -0.2, 8.0 / 315.0, -1.0 / 560.0)
CENTER_COEF = -205.0 / 72.0
FIRST_SCALE = 840
SECOND_SCALE = 5040
DIFFUSIVITY = (0.05, 0.04, 0.03, 0.08)
TIME_STEP = 0.2
RATE_CONST = 2.0
IGNITION_SLOPE = 8.0
IGNITION_TEMP = 0.5
OXIDIZER_RATIO = 1.5
HEAT_RELEASE = 0.8
SHEAR_CELLS = 2.0
OPACITY_TOTAL = 6.0
SOURCE_COEF = (-1.0, -OXIDIZER_RATIO, 1.0 + OXIDIZER_RATIO, HEAT_RELEASE)

VMEM_LIMIT = 24 * 1024 * 1024
F32 = jnp.float32
BF16 = jnp.bfloat16


def halves(value):
    upper = value.astype(BF16)
    return upper, (value - upper.astype(F32)).astype(BF16)


def by_field(field, values):
    result = jnp.float32(values[-1])
    for index in range(len(values) - 2, -1, -1):
        result = jnp.where(field == index, jnp.float32(values[index]), result)
    return result


def pack_field(source, field, depth_out, low_out, high_out, column_out):
    _, depth, rows, columns = source.shape
    half = depth // 2
    depth_out[field, 0:HALO] = source[field, depth - HALO : depth]
    depth_out[field, HALO : 2 * HALO] = source[field, 0:HALO]
    for d in range(half):
        low_out[field, d, 0:HALO] = source[field, d, 0:HALO]
        low_out[field, d, HALO : 2 * HALO] = source[field, d + half, 0:HALO]
        high_out[field, d, 0:HALO] = source[field, d, rows - HALO : rows]
        high_out[field, d, HALO : 2 * HALO] = source[field, d + half, rows - HALO : rows]
    lane = lax.broadcasted_iota(jnp.int32, (rows, columns), 1)
    packed = jnp.zeros((rows, columns), F32)
    for d in range(depth):
        turned = pltpu.roll(source[field, d], (2 * HALO * d + HALO) % columns, 1)
        packed = jnp.where(lane // (2 * HALO) == d, turned, packed)
    column_out[field] = packed


def pack_kernel(
    state_in, velocity_in, table_in, depth_out, low_out, high_out, column_out, state, velocity, table, sems
):
    copies = [
        pltpu.make_async_copy(source, target, sems.at[i])
        for i, (source, target) in enumerate(
            ((state_in, state), (velocity_in, velocity), (table_in, table))
        )
    ]
    for copy in copies:
        copy.start()
    copies[0].wait()

    def each(field, carry):
        pack_field(state, field, depth_out, low_out, high_out, column_out)
        return carry

    lax.fori_loop(0, state.shape[0], each, 0)
    for copy in copies[1:]:
        copy.wait()


def reaction(fields, rate):
    rate[...] = (
        RATE_CONST
        * fields[0]
        * fields[1]
        / (1.0 + jnp.exp(-IGNITION_SLOPE * (fields[3] - IGNITION_TEMP)))
    )


def band(cells, columns):
    lane = lax.broadcasted_iota(jnp.int32, cells.shape, 1)
    apart = cells - lane % columns
    distance = jnp.abs(apart)
    first = jnp.zeros(cells.shape, F32)
    second = jnp.zeros(cells.shape, F32)
    for k in range(HALO):
        near = distance == k + 1
        first = jnp.where(near, float(round(FIRST_COEF[k] * FIRST_SCALE)), first)
        second = jnp.where(near, float(round(SECOND_COEF[k] * SECOND_SCALE)), second)
    first = jnp.where(apart < 0, -first, first)
    return jnp.where(lane < columns, first, second).astype(BF16)


def interior_field(fields, field, velocity, inner_weight, rate, padded, across, write):
    _, depth, rows, columns = fields.shape
    start = 2 * HALO
    upper, lower = halves(fields[field].reshape(depth * rows, columns))
    across[...] = jnp.dot(
        jnp.concatenate([upper, lower], 1), inner_weight[...], preferred_element_type=F32
    )
    for d in range(depth):
        padded[d, start : start + rows] = fields[field, d]
    diffusivity = by_field(field, DIFFUSIVITY)
    source = by_field(field, SOURCE_COEF)
    for d in range(depth):
        centre = fields[field, d]
        laplace = 3.0 * CENTER_COEF * centre
        along_depth = jnp.zeros_like(centre)
        along_row = jnp.zeros_like(centre)
        for k in range(HALO):
            up = padded[d, start + k + 1 : start + k + 1 + rows]
            down = padded[d, start - k - 1 : start - k - 1 + rows]
            along_row = along_row + FIRST_COEF[k] * (up - down)
            both = up + down
            if d + k + 1 < depth:
                ahead = fields[field, d + k + 1]
                along_depth = along_depth + FIRST_COEF[k] * ahead
                both = both + ahead
            if d - k - 1 >= 0:
                behind = fields[field, d - k - 1]
                along_depth = along_depth - FIRST_COEF[k] * behind
                both = both + behind
            laplace = laplace + SECOND_COEF[k] * both
        here = pl.ds(d * rows, rows)
        along_column = across[here, 0:columns] * (1.0 / FIRST_SCALE)
        laplace = laplace + across[here, columns : 2 * columns] * (1.0 / SECOND_SCALE)
        advect = (
            velocity[0, d] * along_depth
            + velocity[1, d] * along_row
            + velocity[2, d] * along_column
        )
        write(d, diffusivity * laplace - advect + source * rate[d])


def halo_field(part, field, velocity, halos, halo_weight, below, above, across, scale, write):
    depth_halo, row_below, row_above, column_below, column_above = halos
    depth, rows, columns = velocity.shape[1:]
    half = depth // 2
    lane = lax.broadcasted_iota(jnp.int32, (rows, columns), 1)
    edge = jnp.where(lane % (2 * HALO) < HALO, column_below[field], column_above[field])
    edge_upper, edge_lower = halves(edge)
    spread = []
    for d in range(depth):
        own = lane // (2 * HALO) == d
        zero = jnp.zeros((rows, columns), BF16)
        spread.append(
            jnp.concatenate(
                [jnp.where(own, edge_upper, zero), jnp.where(own, edge_lower, zero)], 1
            )
        )
    across[...] = jnp.dot(
        jnp.concatenate(spread, 0), halo_weight[...], preferred_element_type=F32
    )
    for d in range(depth):
        piece = slice(0, HALO) if d < half else slice(HALO, 2 * HALO)
        below[d, HALO : 2 * HALO] = row_below[field, d % half, piece]
        above[d, 2 * HALO : 3 * HALO] = row_above[field, d % half, piece]
    diffusivity = by_field(field, DIFFUSIVITY)
    block = 2 * HALO
    for d in range(depth):
        value = []
        for first in range(0, rows, block):
            here = slice(first, first + block)
            along_column = across[pl.ds(d * rows + first, block), 0:columns] * (1.0 / FIRST_SCALE)
            laplace = across[pl.ds(d * rows + first, block), columns : 2 * columns] * (
                1.0 / SECOND_SCALE
            )
            advect = velocity[2, d, here] * along_column
            along_row = None
            for k in range(HALO):
                if first == 0:
                    down = below[d, block - k - 1 : 2 * block - k - 1]
                    term = -FIRST_COEF[k] * down
                    along_row = term if along_row is None else along_row + term
                    laplace = laplace + SECOND_COEF[k] * down
                if first + block == rows:
                    up = above[d, k + 1 : k + 1 + block]
                    term = FIRST_COEF[k] * up
                    along_row = term if along_row is None else along_row + term
                    laplace = laplace + SECOND_COEF[k] * up
            if along_row is not None:
                advect = advect + velocity[1, d, here] * along_row
            along_depth = None
            for k in range(HALO):
                if d - k - 1 < 0:
                    behind = depth_halo[field, d - k - 1 + HALO, here]
                    term = -FIRST_COEF[k] * behind
                    along_depth = term if along_depth is None else along_depth + term
                    laplace = laplace + SECOND_COEF[k] * behind
                if d + k + 1 >= depth:
                    ahead = depth_halo[field, d + k + 1 - depth + HALO, here]
                    term = FIRST_COEF[k] * ahead
                    along_depth = term if along_depth is None else along_depth + term
                    laplace = laplace + SECOND_COEF[k] * ahead
            if along_depth is not None:
                advect = advect + velocity[0, d, here] * along_depth
            write(d, here, part[field, d, here] + scale * (diffusivity * laplace - advect))


def first_interior(
    slice_total,
    state,
    velocity,
    table,
    columns_sent,
    part,
    inner_weight,
    halo_weight,
    row_weight,
    column_weight,
    packed_table,
    rate,
    padded,
    across,
):
    del columns_sent
    _, depth, rows, columns = state.shape
    shape = inner_weight.shape
    index = lax.broadcasted_iota(jnp.int32, shape, 0) % columns
    inner_weight[...] = band(index, columns)
    edge = index % (2 * HALO)
    halo_weight[...] = band(jnp.where(edge < HALO, edge, edge + columns) - HALO, columns)
    shape = column_weight.shape
    cell = (lax.broadcasted_iota(jnp.int32, shape, 0) % columns).astype(F32)
    pixel = (lax.broadcasted_iota(jnp.int32, shape, 1) % PIX_C).astype(F32)
    column_weight[...] = tent(pixel, cell, 0.0, columns, PIX_C).astype(BF16)
    half = depth // 2
    place = lax.axis_index("depth") * depth
    shape = (PIX_R, row_weight.shape[2])
    pixel = lax.broadcasted_iota(jnp.int32, shape, 0).astype(F32)
    lane = lax.broadcasted_iota(jnp.int32, shape, 1)
    cell = (lane % rows).astype(F32)
    later = (lane // rows % 2) * half
    for i in range(half):
        level = (place + i + later).astype(F32)
        shift = SHEAR_CELLS * ((level + 0.5) / slice_total - 0.5)
        row_weight[i] = tent(pixel, cell, shift, rows, PIX_R).astype(BF16)
    levels = table.shape[1]
    packed = table[0:1] + table[1:2] * 256 + table[2:3] * 65536 + table[3:4] * 16777216
    packed_table[0:1] = packed
    packed_table[1:2] = jnp.concatenate([packed[:, 1:], packed[:, levels - 1 :]], 1)
    padded[...] = jnp.zeros_like(padded)
    reaction(state, rate)

    def each(field, carry):
        def write(d, value):
            part[field, d] = state[field, d] + TIME_STEP * value

        interior_field(state, field, velocity, inner_weight, rate, padded, across, write)
        return carry

    lax.fori_loop(0, state.shape[0], each, 0)


def first_halo(
    part,
    velocity,
    depth_halo,
    row_below,
    row_above,
    column_below,
    column_above,
    halo_weight,
    middle,
    depth_out,
    low_out,
    high_out,
    column_out,
    below,
    above,
    across,
):
    halos = (depth_halo, row_below, row_above, column_below, column_above)
    below[...] = jnp.zeros_like(below)
    above[...] = jnp.zeros_like(above)

    def each(field, carry):
        def write(d, here, value):
            middle[field, d, here] = value

        halo_field(
            part, field, velocity, halos, halo_weight, below, above, across, TIME_STEP, write
        )
        pack_field(middle, field, depth_out, low_out, high_out, column_out)
        return carry

    lax.fori_loop(0, part.shape[0], each, 0)


def second_interior(
    middle, state, velocity, inner_weight, columns_sent, part, rate, padded, across
):
    del columns_sent
    padded[...] = jnp.zeros_like(padded)
    reaction(middle, rate)

    def each(field, carry):
        def write(d, value):
            part[field, d] = 0.5 * (state[field, d] + middle[field, d]) + (
                0.5 * TIME_STEP
            ) * value

        interior_field(middle, field, velocity, inner_weight, rate, padded, across, write)
        return carry

    lax.fori_loop(0, state.shape[0], each, 0)


def tent(pixel, cell, shift, cells, pixels):
    stride = cells / pixels
    reach = max(1.0, stride)
    at = jnp.clip((pixel + 0.5) * stride - 0.5 + shift, 0.0, cells - 1.0)
    return jnp.maximum(0.0, 1.0 - jnp.abs(at - cell) / reach) / reach


def sample_slices(temperature, column_weight, row_weight, samples):
    depth, rows, columns = temperature.shape
    half = depth // 2
    upper, lower = halves(temperature[...].reshape(depth * rows, columns))
    wide = jnp.dot(
        jnp.concatenate([upper, lower], 1), column_weight[...], preferred_element_type=F32
    )
    lane = lax.broadcasted_iota(jnp.int32, (rows, 2 * PIX_C), 1)
    for i in range(half):
        left = jnp.where(lane < PIX_C, wide[i * rows : (i + 1) * rows], 0.0)
        right = jnp.where(
            lane < PIX_C, 0.0, wide[(i + half) * rows : (i + half + 1) * rows]
        )
        both_upper, both_lower = halves(jnp.concatenate([left, right], 0))
        samples[i] = jnp.dot(
            row_weight[i],
            jnp.concatenate([both_upper, both_lower], 0),
            preferred_element_type=F32,
        )


def look_up(tables, index, shape):
    lanes = tables[0].shape[1]
    inside = index % lanes
    result = None
    for part, table in enumerate(tables):
        found = jnp.take_along_axis(
            jnp.broadcast_to(table, shape), inside, axis=1, mode="promise_in_bounds"
        )
        result = found if part == 0 else jnp.where(index >= part * lanes, found, result)
    return result


def march(samples, table, flag, slice_total, share):
    half, pixel_rows, lanes = samples.shape
    levels = table.shape[1]
    below_tables = [table[0:1, i : i + lanes] for i in range(0, levels, lanes)]
    above_tables = [table[1:2, i : i + lanes] for i in range(0, levels, lanes)]
    shape = (pixel_rows // 2, lanes)
    lane = lax.broadcasted_iota(jnp.int32, shape, 1)
    in_front = (lane < PIX_C) == (flag == 0)
    parts = []
    for part in range(2):
        rows_here = pl.ds(part * shape[0], shape[0])

        def advance(position, running):
            chosen = jnp.where(flag == 0, half - 1 - position, position)
            values = samples[chosen, rows_here]
            level = jnp.clip(values, 0.0, 1.0) * (levels - 1.0)
            lower = jnp.minimum(level.astype(jnp.int32), levels - 2)
            fraction = level - lower.astype(F32)
            below = look_up(below_tables, lower, shape)
            above = look_up(above_tables, lower, shape)
            raw = []
            for channel in range(4):
                low = (lax.shift_right_logical(below, 8 * channel) & 255).astype(F32)
                high = (lax.shift_right_logical(above, 8 * channel) & 255).astype(F32)
                raw.append(low + fraction * (high - low))
            alpha = raw[3] * (OPACITY_TOTAL / slice_total / 255.0)
            scaled = alpha * (1.0 / 255.0)
            through = 1.0 - alpha
            return tuple(
                [scaled * raw[c] + through * running[c] for c in range(3)]
                + [alpha + through * running[3]]
            )

        zero = jnp.zeros(shape, F32)
        parts.append(lax.fori_loop(0, half, advance, (zero, zero, zero, zero)))
    for channel in range(4):
        merged = []
        for part in range(2):
            own, own_alpha = parts[part][channel], parts[part][3]
            other, other_alpha = pltpu.roll(own, PIX_C, 1), pltpu.roll(own_alpha, PIX_C, 1)
            merged.append(
                jnp.where(
                    in_front, own + (1.0 - own_alpha) * other, other + (1.0 - other_alpha) * own
                )
            )
        share[channel] = jnp.where(lane < PIX_C, merged[0], merged[1])


def temperature_halo(
    slice_total,
    order,
    part,
    velocity,
    depth_halo,
    row_below,
    row_above,
    column_below,
    column_above,
    halo_weight,
    column_weight,
    row_weight,
    table,
    temperature,
    share,
    toward,
    below,
    above,
    across,
    samples,
):
    halos = (depth_halo, row_below, row_above, column_below, column_above)
    below[...] = jnp.zeros_like(below)
    above[...] = jnp.zeros_like(above)

    def write(d, here, value):
        temperature[d, here] = value

    halo_field(
        part, 3, velocity, halos, halo_weight, below, above, across, 0.5 * TIME_STEP, write
    )
    sample_slices(temperature, column_weight, row_weight, samples)
    toward[...] = jnp.full(toward.shape, order[0, 0], jnp.int32)
    march(samples, table, order[0, 0], slice_total, share)


def fractions_halo(
    part,
    temperature,
    velocity,
    depth_halo,
    row_below,
    row_above,
    column_below,
    column_above,
    halo_weight,
    share,
    new_state,
    below,
    above,
    across,
):
    del share
    halos = (depth_halo, row_below, row_above, column_below, column_above)
    below[...] = jnp.zeros_like(below)
    above[...] = jnp.zeros_like(above)

    def each(field, carry):
        def write(d, here, value):
            new_state[field, d, here] = value

        halo_field(
            part, field, velocity, halos, halo_weight, below, above, across, 0.5 * TIME_STEP, write
        )
        return carry

    lax.fori_loop(0, 3, each, 0)
    new_state[3] = temperature[...]


def merge_kernel(bit, last, toward, own, received, out):
    shape = own.shape[1:]
    mine = lax.axis_index("depth") // 2**bit % 2
    front = jnp.broadcast_to(toward[0:1] == mine, shape)
    own_alpha, received_alpha = own[3], received[3]
    for channel in range(4):
        one, two = own[channel], received[channel]
        front_value = one + (1.0 - own_alpha) * two
        back_value = two + (1.0 - received_alpha) * one
        value = jnp.where(front, front_value, back_value)
        if last:
            out[channel, 0 : shape[0]] = value[:, 0:PIX_C]
            out[channel, shape[0] : 2 * shape[0]] = pltpu.roll(value, PIX_C, 1)[:, 0:PIX_C]
        else:
            out[channel] = value


def shift(value, axis, step):
    count = lax.axis_size(axis)
    return lax.ppermute(value, axis, [(i, (i + step) % count) for i in range(count)])


def exchange(depth_faces, low_rows, high_rows, columns):
    if lax.axis_size("depth") == 2:
        depth_halo = shift(depth_faces, "depth", 1)
    else:
        depth_halo = jnp.concatenate(
            [
                shift(depth_faces[:, :HALO], "depth", 1),
                shift(depth_faces[:, HALO:], "depth", -1),
            ],
            1,
        )
    row_below = shift(high_rows, "row", 1)
    row_above = shift(low_rows, "row", -1)
    column_below = shift(columns, "col", 1)
    column_above = shift(columns, "col", -1)
    return depth_halo, row_below, row_above, column_below, column_above


def call(kernel, outs, scratch, specs, *args):
    vmem = pl.BlockSpec(memory_space=pltpu.VMEM)
    return pl.pallas_call(
        kernel,
        out_shape=outs,
        in_specs=specs + [vmem] * (len(args) - len(specs)),
        out_specs=jax.tree.map(lambda _: vmem, outs),
        scratch_shapes=scratch,
        compiler_params=pltpu.CompilerParams(vmem_limit_bytes=VMEM_LIMIT),
    )(*args)


def in_hbm(value):
    return pltpu.with_memory_space_constraint(value, pltpu.HBM)


def local(state, velocity, view_order, tf_table):
    fields, depth, rows, columns = state.shape
    depth_count = lax.axis_size("depth")

    def array(*shape, dtype=F32):
        return jax.ShapeDtypeStruct(shape, dtype)

    whole = array(*state.shape)
    faces = (
        array(fields, 2 * HALO, rows, columns),
        array(fields, depth // 2, 2 * HALO, columns),
        array(fields, depth // 2, 2 * HALO, columns),
        array(fields, rows, columns),
    )
    across = pltpu.VMEM((depth * rows, 2 * columns), F32)
    inner_work = [
        pltpu.VMEM((depth, rows, columns), F32),
        pltpu.VMEM((depth, rows + 4 * HALO, columns), F32),
        across,
    ]
    halo_work = [
        pltpu.VMEM((depth, 4 * HALO, columns), F32),
        pltpu.VMEM((depth, 4 * HALO, columns), F32),
        across,
    ]
    slice_total = depth * depth_count

    hbm = pl.BlockSpec(memory_space=pltpu.HBM)
    *sent, state, velocity, table = call(
        pack_kernel,
        faces + (whole, array(*velocity.shape), array(*tf_table.shape, dtype=jnp.int32)),
        [pltpu.SemaphoreType.DMA((3,))],
        [hbm, hbm, hbm],
        in_hbm(state),
        in_hbm(velocity),
        in_hbm(tf_table),
    )
    halos = exchange(*sent)
    part, inner_weight, halo_weight, row_weight, column_weight, table = call(
        functools.partial(first_interior, slice_total),
        (
            whole,
            array(2 * columns, 2 * columns, dtype=BF16),
            array(2 * columns, 2 * columns, dtype=BF16),
            array(depth // 2, PIX_R, 4 * rows, dtype=BF16),
            array(2 * columns, 2 * PIX_C, dtype=BF16),
            array(2, tf_table.shape[1], dtype=jnp.int32),
        ),
        inner_work,
        [],
        state,
        velocity,
        table,
        sent[3],
    )
    middle, *sent = call(
        first_halo, (whole,) + faces, halo_work, [], part, velocity, *halos, halo_weight
    )
    halos = exchange(*sent)
    part = call(
        second_interior,
        whole,
        inner_work,
        [],
        middle,
        state,
        velocity,
        inner_weight,
        sent[3],
    )
    temperature, share, toward = call(
        functools.partial(temperature_halo, slice_total),
        (
            array(depth, rows, columns),
            array(4, PIX_R // 2, 2 * PIX_C),
            array(8, 2 * PIX_C, dtype=jnp.int32),
        ),
        halo_work
        + [pltpu.VMEM((depth // 2, PIX_R, 2 * PIX_C), F32)],
        [pl.BlockSpec(memory_space=pltpu.SMEM)],
        view_order,
        part,
        velocity,
        *halos,
        halo_weight,
        column_weight,
        row_weight,
        table,
    )
    new_state = call(
        fractions_halo,
        whole,
        halo_work,
        [],
        part,
        temperature,
        velocity,
        *halos,
        halo_weight,
        share,
    )
    bits = depth_count.bit_length() - 1
    for bit in range(bits):
        pairs = [(i, i ^ 2**bit) for i in range(depth_count)]
        received = lax.ppermute(share, "depth", pairs)
        last = bit == bits - 1
        share = call(
            functools.partial(merge_kernel, bit, last),
            array(4, PIX_R, PIX_C) if last else array(*share.shape),
            [],
            [],
            toward,
            share,
            received,
        )
    return new_state, share


def solution(mesh):
    in_specs = (
        P(None, "depth", "row", "col"),
        P(None, "depth", "row", "col"),
        P("row", "col"),
        P(),
    )
    out_specs = (P(None, "depth", "row", "col"), P(None, "row", "col"))
    return jax.shard_map(local, mesh=mesh, in_specs=in_specs, out_specs=out_specs, check_vma=False)
```

```python
import functools

import jax
import jax.numpy as jnp
from jax import lax
from jax.experimental import pallas as pl
from jax.experimental.pallas import tpu as pltpu
from jax.sharding import PartitionSpec as P

PIX_R = 64
PIX_C = 64
HALO = 4

FIRST_COEF = (0.8, -0.2, 4.0 / 105.0, -1.0 / 280.0)
SECOND_COEF = (1.6, -0.2, 8.0 / 315.0, -1.0 / 560.0)
CENTER_COEF = -205.0 / 72.0
FIRST_SCALE = 840
SECOND_SCALE = 5040
DIFFUSIVITY = (0.05, 0.04, 0.03, 0.08)
TIME_STEP = 0.2
RATE_CONST = 2.0
IGNITION_SLOPE = 8.0
IGNITION_TEMP = 0.5
OXIDIZER_RATIO = 1.5
HEAT_RELEASE = 0.8
SHEAR_CELLS = 2.0
OPACITY_TOTAL = 6.0
SOURCE_COEF = (-1.0, -OXIDIZER_RATIO, 1.0 + OXIDIZER_RATIO, HEAT_RELEASE)

VMEM_LIMIT = 24 * 1024 * 1024
F32 = jnp.float32
BF16 = jnp.bfloat16


def halves(value):
    upper = value.astype(BF16)
    return upper, (value - upper.astype(F32)).astype(BF16)


def by_field(field, values):
    result = jnp.float32(values[-1])
    for index in range(len(values) - 2, -1, -1):
        result = jnp.where(field == index, jnp.float32(values[index]), result)
    return result


def pack_rows(layers, low_out, high_out):
    depth, rows, _ = layers.shape
    half = depth // 2
    for d in range(half):
        low_out[d, 0:HALO] = layers[d, 0:HALO]
        low_out[d, HALO : 2 * HALO] = layers[d + half, 0:HALO]
        high_out[d, 0:HALO] = layers[d, rows - HALO : rows]
        high_out[d, HALO : 2 * HALO] = layers[d + half, rows - HALO : rows]


def pack_columns(layers, out):
    depth, rows, columns = layers.shape
    lane = lax.broadcasted_iota(jnp.int32, (rows, columns), 1)
    packed = jnp.zeros((rows, columns), F32)
    for d in range(depth):
        turned = pltpu.roll(layers[d], (2 * HALO * d + HALO) % columns, 1)
        packed = jnp.where(lane // (2 * HALO) == d, turned, packed)
    out[...] = packed


def pack_field(source, field, depth_out, low_out, high_out, column_out):
    depth = source.shape[1]
    depth_out[field, 0:HALO] = source[field, depth - HALO : depth]
    depth_out[field, HALO : 2 * HALO] = source[field, 0:HALO]
    pack_rows(source.at[field], low_out.at[field], high_out.at[field])
    pack_columns(source.at[field], column_out.at[field])


def pack_kernel(
    state_in,
    velocity_in,
    table_in,
    depth_out,
    low_out,
    high_out,
    column_out,
    state,
    velocity,
    table,
    sems,
):
    fields, depth = state.shape[:2]
    outer = depth - HALO
    pairs = [(state_in.at[field], state.at[field]) for field in range(fields)]
    pairs += [
        (state_in.at[:, outer:depth], depth_out.at[:, 0:HALO]),
        (state_in.at[:, 0:HALO], depth_out.at[:, HALO : 2 * HALO]),
        (velocity_in, velocity),
        (table_in, table),
    ]
    copies = [
        pltpu.make_async_copy(source, target, sems.at[i])
        for i, (source, target) in enumerate(pairs)
    ]
    for copy in copies:
        copy.start()
    for field in range(fields):
        copies[field].wait()
        pack_rows(state.at[field], low_out.at[field], high_out.at[field])
        pack_columns(state.at[field], column_out.at[field])
    for copy in copies[fields:]:
        copy.wait()


def reaction(fields, rate):
    rate[...] = (
        RATE_CONST
        * fields[0]
        * fields[1]
        / (1.0 + jnp.exp(-IGNITION_SLOPE * (fields[3] - IGNITION_TEMP)))
    )


def band(cells, targets, columns):
    lane = lax.broadcasted_iota(jnp.int32, cells.shape, 1)
    apart = cells - targets
    distance = jnp.abs(apart)
    first = jnp.zeros(cells.shape, F32)
    second = jnp.zeros(cells.shape, F32)
    for k in range(HALO):
        near = distance == k + 1
        first = jnp.where(near, float(round(FIRST_COEF[k] * FIRST_SCALE)), first)
        second = jnp.where(near, float(round(SECOND_COEF[k] * SECOND_SCALE)), second)
    first = jnp.where(apart < 0, -first, first)
    return jnp.where(lane < columns, first, second).astype(BF16)


def interior_field(fields, field, velocity, inner_weight, rate, padded, across, write):
    _, depth, rows, columns = fields.shape
    start = 2 * HALO
    upper, lower = halves(fields[field].reshape(depth * rows, columns))
    across[...] = jnp.dot(
        jnp.concatenate([upper, lower], 1), inner_weight[...], preferred_element_type=F32
    )
    for d in range(depth):
        padded[d, start : start + rows] = fields[field, d]
    diffusivity = by_field(field, DIFFUSIVITY)
    source = by_field(field, SOURCE_COEF)
    for d in range(depth):
        centre = fields[field, d]
        laplace = 3.0 * CENTER_COEF * centre
        along_depth = jnp.zeros_like(centre)
        along_row = jnp.zeros_like(centre)
        for k in range(HALO):
            up = padded[d, start + k + 1 : start + k + 1 + rows]
            down = padded[d, start - k - 1 : start - k - 1 + rows]
            along_row = along_row + FIRST_COEF[k] * (up - down)
            both = up + down
            if d + k + 1 < depth:
                ahead = fields[field, d + k + 1]
                along_depth = along_depth + FIRST_COEF[k] * ahead
                both = both + ahead
            if d - k - 1 >= 0:
                behind = fields[field, d - k - 1]
                along_depth = along_depth - FIRST_COEF[k] * behind
                both = both + behind
            laplace = laplace + SECOND_COEF[k] * both
        here = pl.ds(d * rows, rows)
        along_column = across[here, 0:columns] * (1.0 / FIRST_SCALE)
        laplace = laplace + across[here, columns : 2 * columns] * (1.0 / SECOND_SCALE)
        advect = (
            velocity[0, d] * along_depth
            + velocity[1, d] * along_row
            + velocity[2, d] * along_column
        )
        write(d, diffusivity * laplace - advect + source * rate[d])


def halo_fields(part, fields, velocity, edge_velocity, halos, halo_weight, scale, write):
    depth_halo, row_below, row_above, column_below, column_above = halos
    low_velocity, high_velocity, column_velocity = edge_velocity
    depth, rows, columns = velocity.shape[1:]
    half = depth // 2
    block = 2 * HALO
    lane = lax.broadcasted_iota(jnp.int32, (rows, columns), 1)
    behind_lane = lane % block < HALO
    edges = jnp.concatenate(
        [jnp.where(behind_lane, column_below[f], column_above[f]) for f in fields], 0
    )
    upper, lower = halves(edges)
    along = jnp.dot(
        jnp.concatenate([upper, lower], 1), halo_weight[...], preferred_element_type=F32
    )
    along_columns = []
    for n, field in enumerate(fields):
        mine = along[n * rows : (n + 1) * rows]
        along_columns.append(
            mine[:, columns:] * (scale * DIFFUSIVITY[field] / SECOND_SCALE)
            - (column_velocity[...] * (scale / FIRST_SCALE)) * mine[:, :columns]
        )

    tile = (block, columns)
    sublane = lax.broadcasted_iota(jnp.int32, tile, 0)
    lane = lax.broadcasted_iota(jnp.int32, tile, 1)
    outer_lane = (lane < HALO) | (lane >= columns - HALO)
    early = sublane < HALO
    step = sublane % HALO
    below_first, below_second, above_first, above_second = [], [], [], []
    for s in range(HALO):
        first, second = FIRST_COEF[HALO - 1 - s], SECOND_COEF[HALO - 1 - s]
        below_first.append(jnp.where(step + s < HALO, -scale * first, 0.0))
        below_second.append(jnp.where(step + s < HALO, scale * second, 0.0))
        above_first.append(jnp.where(step >= s, scale * first, 0.0))
        above_second.append(jnp.where(step >= s, scale * second, 0.0))

    def edge_rows(halo, direction, first_weights, second_weights, speed, diffusivity):
        first = second = None
        for s in range(HALO):
            turned = halo if s == 0 else pltpu.roll(halo, (direction * s) % block, 0)
            one, two = first_weights[s] * turned, second_weights[s] * turned
            first = one if first is None else first + one
            second = two if second is None else second + two
        return diffusivity * second - speed * first

    for n, field in enumerate(fields):
        diffusivity = DIFFUSIVITY[field]
        for i in range(half):
            low = edge_rows(
                row_below[field, i], -1, below_first, below_second, low_velocity[i], diffusivity
            )
            high = edge_rows(
                row_above[field, i], 1, above_first, above_second, high_velocity[i], diffusivity
            )
            for d in (i, i + half):
                low_here = low if d < half else pltpu.roll(low, HALO, 0)
                high_here = pltpu.roll(high, HALO, 0) if d < half else high
                for first_row in range(0, rows, block):
                    here = slice(first_row, first_row + block)
                    value = part[field, d, here]
                    if first_row == 0:
                        value = value + jnp.where(early, low_here, 0.0)
                    if first_row + block == rows:
                        value = value + jnp.where(early, 0.0, high_here)
                    turned = pltpu.roll(
                        along_columns[n][here], (-block * d - HALO) % columns, 1
                    )
                    value = value + jnp.where(outer_lane, turned, 0.0)
                    terms = [(-1, d - k - 1 + HALO, k) for k in range(HALO) if d - k - 1 < 0]
                    terms += [
                        (1, d + k + 1 - depth + HALO, k)
                        for k in range(HALO)
                        if d + k + 1 >= depth
                    ]
                    first = second = None
                    for sign, layer, k in terms:
                        cells = depth_halo[field, layer, here]
                        one = (sign * scale * FIRST_COEF[k]) * cells
                        two = (scale * diffusivity * SECOND_COEF[k]) * cells
                        first = one if first is None else first + one
                        second = two if second is None else second + two
                    if terms:
                        value = value + (second - velocity[0, d, here] * first)
                    write(field, d, here, value)


def first_interior(
    slice_total,
    state,
    velocity,
    table,
    columns_sent,
    part,
    inner_weight,
    halo_weight,
    row_weight,
    column_weight,
    packed_table,
    low_velocity,
    high_velocity,
    column_velocity,
    rate,
    padded,
    across,
):
    del columns_sent
    _, depth, rows, columns = state.shape
    shape = inner_weight.shape
    index = lax.broadcasted_iota(jnp.int32, shape, 0) % columns
    target = lax.broadcasted_iota(jnp.int32, shape, 1) % columns
    inner_weight[...] = band(index, target, columns)
    edge, target_edge = index % (2 * HALO), target % (2 * HALO)
    weight = band(
        jnp.where(edge < HALO, edge, edge + columns) - HALO,
        jnp.where(target_edge < HALO, target_edge + columns, target_edge) - HALO,
        columns,
    )
    same_layer = index // (2 * HALO) == target // (2 * HALO)
    halo_weight[...] = jnp.where(same_layer, weight, jnp.zeros_like(weight))
    pack_rows(velocity.at[1], low_velocity, high_velocity)
    pack_columns(velocity.at[2], column_velocity)
    shape = column_weight.shape
    cell = (lax.broadcasted_iota(jnp.int32, shape, 0) % columns).astype(F32)
    pixel = (lax.broadcasted_iota(jnp.int32, shape, 1) % PIX_C).astype(F32)
    column_weight[...] = tent(pixel, cell, 0.0, columns, PIX_C).astype(BF16)
    half = depth // 2
    place = lax.axis_index("depth") * depth
    shape = (PIX_R, row_weight.shape[2])
    pixel = lax.broadcasted_iota(jnp.int32, shape, 0).astype(F32)
    lane = lax.broadcasted_iota(jnp.int32, shape, 1)
    cell = (lane % rows).astype(F32)
    later = (lane // rows % 2) * half
    for i in range(half):
        level = (place + i + later).astype(F32)
        shift = SHEAR_CELLS * ((level + 0.5) / slice_total - 0.5)
        row_weight[i] = tent(pixel, cell, shift, rows, PIX_R).astype(BF16)
    levels = table.shape[1]
    packed = table[0:1] + table[1:2] * 256 + table[2:3] * 65536 + table[3:4] * 16777216
    packed_table[0:1] = packed
    packed_table[1:2] = jnp.concatenate([packed[:, 1:], packed[:, levels - 1 :]], 1)
    padded[...] = jnp.zeros_like(padded)
    reaction(state, rate)

    def each(field, carry):
        def write(d, value):
            part[field, d] = state[field, d] + TIME_STEP * value

        interior_field(state, field, velocity, inner_weight, rate, padded, across, write)
        return carry

    lax.fori_loop(0, state.shape[0], each, 0)


def first_halo(
    part,
    velocity,
    low_velocity,
    high_velocity,
    column_velocity,
    depth_halo,
    row_below,
    row_above,
    column_below,
    column_above,
    halo_weight,
    middle,
    depth_out,
    low_out,
    high_out,
    column_out,
):
    halos = (depth_halo, row_below, row_above, column_below, column_above)
    edge_velocity = (low_velocity, high_velocity, column_velocity)

    def write(field, d, here, value):
        middle[field, d, here] = value

    fields = range(part.shape[0])
    halo_fields(part, fields, velocity, edge_velocity, halos, halo_weight, TIME_STEP, write)
    for field in fields:
        pack_field(middle, field, depth_out, low_out, high_out, column_out)


def second_interior(
    middle, state, velocity, inner_weight, columns_sent, part, rate, padded, across
):
    del columns_sent
    padded[...] = jnp.zeros_like(padded)
    reaction(middle, rate)

    def each(field, carry):
        def write(d, value):
            part[field, d] = 0.5 * (state[field, d] + middle[field, d]) + (
                0.5 * TIME_STEP
            ) * value

        interior_field(middle, field, velocity, inner_weight, rate, padded, across, write)
        return carry

    lax.fori_loop(0, state.shape[0], each, 0)


def tent(pixel, cell, shift, cells, pixels):
    stride = cells / pixels
    reach = max(1.0, stride)
    at = jnp.clip((pixel + 0.5) * stride - 0.5 + shift, 0.0, cells - 1.0)
    return jnp.maximum(0.0, 1.0 - jnp.abs(at - cell) / reach) / reach


def sample_slices(temperature, column_weight, row_weight, samples):
    depth, rows, columns = temperature.shape
    half = depth // 2
    upper, lower = halves(temperature[...].reshape(depth * rows, columns))
    wide = jnp.dot(
        jnp.concatenate([upper, lower], 1), column_weight[...], preferred_element_type=F32
    )
    lane = lax.broadcasted_iota(jnp.int32, (rows, 2 * PIX_C), 1)
    for i in range(half):
        left = jnp.where(lane < PIX_C, wide[i * rows : (i + 1) * rows], 0.0)
        right = jnp.where(
            lane < PIX_C, 0.0, wide[(i + half) * rows : (i + half + 1) * rows]
        )
        both_upper, both_lower = halves(jnp.concatenate([left, right], 0))
        samples[i] = jnp.dot(
            row_weight[i],
            jnp.concatenate([both_upper, both_lower], 0),
            preferred_element_type=F32,
        )


def look_up(tables, index, shape):
    lanes = tables[0].shape[1]
    inside = index & (lanes - 1)
    result = None
    for part, table in enumerate(tables):
        found = jnp.take_along_axis(
            jnp.broadcast_to(table, shape), inside, axis=1, mode="promise_in_bounds"
        )
        result = found if part == 0 else jnp.where(index >= part * lanes, found, result)
    return result


def march(samples, table, flag, slice_total, share):
    half, pixel_rows, lanes = samples.shape
    levels = table.shape[1]
    below_tables = [table[0:1, i : i + lanes] for i in range(0, levels, lanes)]
    above_tables = [table[1:2, i : i + lanes] for i in range(0, levels, lanes)]
    shape = (pixel_rows // 2, lanes)
    lane = lax.broadcasted_iota(jnp.int32, shape, 1)
    in_front = (lane < PIX_C) == (flag == 0)
    parts = []
    for part in range(2):
        rows_here = pl.ds(part * shape[0], shape[0])

        def advance(position, running):
            chosen = jnp.where(flag == 0, half - 1 - position, position)
            level = jnp.clip(samples[chosen, rows_here] * (levels - 1.0), 0.0, levels - 1.0)
            lower = level.astype(jnp.int32)
            fraction = level - lower.astype(F32)
            below = look_up(below_tables, lower, shape)
            above = look_up(above_tables, lower, shape)
            raw = []
            for channel in range(4):
                low, high = below, above
                if channel > 0:
                    low = lax.shift_right_logical(low, 8 * channel)
                    high = lax.shift_right_logical(high, 8 * channel)
                if channel < 3:
                    low, high = low & 255, high & 255
                low, high = low.astype(F32), high.astype(F32)
                raw.append(low + fraction * (high - low))
            alpha = raw[3] * (OPACITY_TOTAL / slice_total / 255.0)
            through = 1.0 - alpha
            return tuple(
                [alpha * raw[c] + through * running[c] for c in range(3)]
                + [alpha + through * running[3]]
            )

        zero = jnp.zeros(shape, F32)
        running = lax.fori_loop(0, half, advance, (zero, zero, zero, zero), unroll=True)
        parts.append([value * (1.0 / 255.0) for value in running[:3]] + [running[3]])
    for channel in range(4):
        merged = []
        for part in range(2):
            own, own_alpha = parts[part][channel], parts[part][3]
            other, other_alpha = pltpu.roll(own, PIX_C, 1), pltpu.roll(own_alpha, PIX_C, 1)
            merged.append(
                jnp.where(
                    in_front, own + (1.0 - own_alpha) * other, other + (1.0 - other_alpha) * own
                )
            )
        share[channel] = jnp.where(lane < PIX_C, merged[0], merged[1])


def temperature_halo(
    slice_total,
    order,
    part,
    velocity,
    low_velocity,
    high_velocity,
    column_velocity,
    depth_halo,
    row_below,
    row_above,
    column_below,
    column_above,
    halo_weight,
    column_weight,
    row_weight,
    table,
    temperature,
    share,
    toward,
    samples,
):
    halos = (depth_halo, row_below, row_above, column_below, column_above)
    edge_velocity = (low_velocity, high_velocity, column_velocity)

    def write(field, d, here, value):
        temperature[d, here] = value

    halo_fields(part, [3], velocity, edge_velocity, halos, halo_weight, 0.5 * TIME_STEP, write)
    sample_slices(temperature, column_weight, row_weight, samples)
    toward[...] = jnp.full(toward.shape, order[0, 0], jnp.int32)
    march(samples, table, order[0, 0], slice_total, share)


def fractions_halo(
    part,
    temperature,
    velocity,
    low_velocity,
    high_velocity,
    column_velocity,
    depth_halo,
    row_below,
    row_above,
    column_below,
    column_above,
    halo_weight,
    share,
    new_state,
):
    del share
    halos = (depth_halo, row_below, row_above, column_below, column_above)
    edge_velocity = (low_velocity, high_velocity, column_velocity)

    def write(field, d, here, value):
        new_state[field, d, here] = value

    halo_fields(
        part, range(3), velocity, edge_velocity, halos, halo_weight, 0.5 * TIME_STEP, write
    )
    new_state[3] = temperature[...]


def merge_kernel(bit, last, toward, own, received, out):
    shape = own.shape[1:]
    mine = lax.axis_index("depth") // 2**bit % 2
    front = jnp.broadcast_to(toward[0:1] == mine, shape)
    own_alpha, received_alpha = own[3], received[3]
    for channel in range(4):
        one, two = own[channel], received[channel]
        front_value = one + (1.0 - own_alpha) * two
        back_value = two + (1.0 - received_alpha) * one
        value = jnp.where(front, front_value, back_value)
        if last:
            out[channel, 0 : shape[0]] = value[:, 0:PIX_C]
            out[channel, shape[0] : 2 * shape[0]] = pltpu.roll(value, PIX_C, 1)[:, 0:PIX_C]
        else:
            out[channel] = value


def shift(value, axis, step):
    count = lax.axis_size(axis)
    return lax.ppermute(value, axis, [(i, (i + step) % count) for i in range(count)])


def exchange(depth_faces, low_rows, high_rows, columns):
    if lax.axis_size("depth") == 2:
        depth_halo = shift(depth_faces, "depth", 1)
    else:
        depth_halo = jnp.concatenate(
            [
                shift(depth_faces[:, :HALO], "depth", 1),
                shift(depth_faces[:, HALO:], "depth", -1),
            ],
            1,
        )
    row_below = shift(high_rows, "row", 1)
    row_above = shift(low_rows, "row", -1)
    column_below = shift(columns, "col", 1)
    column_above = shift(columns, "col", -1)
    return depth_halo, row_below, row_above, column_below, column_above


def call(kernel, outs, scratch, specs, *args):
    vmem = pl.BlockSpec(memory_space=pltpu.VMEM)
    return pl.pallas_call(
        kernel,
        out_shape=outs,
        in_specs=specs + [vmem] * (len(args) - len(specs)),
        out_specs=jax.tree.map(lambda _: vmem, outs),
        scratch_shapes=scratch,
        compiler_params=pltpu.CompilerParams(vmem_limit_bytes=VMEM_LIMIT),
    )(*args)


def in_hbm(value):
    return pltpu.with_memory_space_constraint(value, pltpu.HBM)


def local(state, velocity, view_order, tf_table):
    fields, depth, rows, columns = state.shape
    depth_count = lax.axis_size("depth")

    def array(*shape, dtype=F32):
        return jax.ShapeDtypeStruct(shape, dtype)

    whole = array(*state.shape)
    faces = (
        array(fields, 2 * HALO, rows, columns),
        array(fields, depth // 2, 2 * HALO, columns),
        array(fields, depth // 2, 2 * HALO, columns),
        array(fields, rows, columns),
    )
    inner_work = [
        pltpu.VMEM((depth, rows, columns), F32),
        pltpu.VMEM((depth, rows + 4 * HALO, columns), F32),
        pltpu.VMEM((depth * rows, 2 * columns), F32),
    ]
    edge_rows = array(depth // 2, 2 * HALO, columns)
    slice_total = depth * depth_count

    hbm = pl.BlockSpec(memory_space=pltpu.HBM)
    *sent, state, velocity, table = call(
        pack_kernel,
        faces + (whole, array(*velocity.shape), array(*tf_table.shape, dtype=jnp.int32)),
        [pltpu.SemaphoreType.DMA((fields + 4,))],
        [hbm, hbm, hbm],
        in_hbm(state),
        in_hbm(velocity),
        in_hbm(tf_table),
    )
    halos = exchange(*sent)
    part, inner_weight, halo_weight, row_weight, column_weight, table, *edge_velocity = call(
        functools.partial(first_interior, slice_total),
        (
            whole,
            array(2 * columns, 2 * columns, dtype=BF16),
            array(2 * columns, 2 * columns, dtype=BF16),
            array(depth // 2, PIX_R, 4 * rows, dtype=BF16),
            array(2 * columns, 2 * PIX_C, dtype=BF16),
            array(2, tf_table.shape[1], dtype=jnp.int32),
            edge_rows,
            edge_rows,
            array(rows, columns),
        ),
        inner_work,
        [],
        state,
        velocity,
        table,
        sent[3],
    )
    middle, *sent = call(
        first_halo,
        (whole,) + faces,
        [],
        [],
        part,
        velocity,
        *edge_velocity,
        *halos,
        halo_weight,
    )
    halos = exchange(*sent)
    part = call(
        second_interior,
        whole,
        inner_work,
        [],
        middle,
        state,
        velocity,
        inner_weight,
        sent[3],
    )
    temperature, share, toward = call(
        functools.partial(temperature_halo, slice_total),
        (
            array(depth, rows, columns),
            array(4, PIX_R // 2, 2 * PIX_C),
            array(8, 2 * PIX_C, dtype=jnp.int32),
        ),
        [pltpu.VMEM((depth // 2, PIX_R, 2 * PIX_C), F32)],
        [pl.BlockSpec(memory_space=pltpu.SMEM)],
        view_order,
        part,
        velocity,
        *edge_velocity,
        *halos,
        halo_weight,
        column_weight,
        row_weight,
        table,
    )
    new_state = call(
        fractions_halo,
        whole,
        [],
        [],
        part,
        temperature,
        velocity,
        *edge_velocity,
        *halos,
        halo_weight,
        share,
    )
    bits = depth_count.bit_length() - 1
    for bit in range(bits):
        pairs = [(i, i ^ 2**bit) for i in range(depth_count)]
        received = lax.ppermute(share, "depth", pairs)
        last = bit == bits - 1
        share = call(
            functools.partial(merge_kernel, bit, last),
            array(4, PIX_R, PIX_C) if last else array(*share.shape),
            [],
            [],
            toward,
            share,
            received,
        )
    return new_state, share


def solution(mesh):
    in_specs = (
        P(None, "depth", "row", "col"),
        P(None, "depth", "row", "col"),
        P("row", "col"),
        P(),
    )
    out_specs = (P(None, "depth", "row", "col"), P(None, "row", "col"))
    return jax.shard_map(local, mesh=mesh, in_specs=in_specs, out_specs=out_specs, check_vma=False)
```

```python
import functools

import jax
import jax.numpy as jnp
from jax import lax
from jax.experimental import pallas as pl
from jax.experimental.pallas import tpu as pltpu
from jax.sharding import PartitionSpec as P

PIX_R = 64
PIX_C = 64
HALO = 4

FIRST_COEF = (0.8, -0.2, 4.0 / 105.0, -1.0 / 280.0)
SECOND_COEF = (1.6, -0.2, 8.0 / 315.0, -1.0 / 560.0)
CENTER_COEF = -205.0 / 72.0
FIRST_SCALE = 840
SECOND_SCALE = 5040
DIFFUSIVITY = (0.05, 0.04, 0.03, 0.08)
TIME_STEP = 0.2
RATE_CONST = 2.0
IGNITION_SLOPE = 8.0
IGNITION_TEMP = 0.5
OXIDIZER_RATIO = 1.5
HEAT_RELEASE = 0.8
SHEAR_CELLS = 2.0
OPACITY_TOTAL = 6.0
SOURCE_COEF = (-1.0, -OXIDIZER_RATIO, 1.0 + OXIDIZER_RATIO, HEAT_RELEASE)

VMEM_LIMIT = 24 * 1024 * 1024
F32 = jnp.float32
BF16 = jnp.bfloat16


def halves(value):
    upper = value.astype(BF16)
    return upper, (value - upper.astype(F32)).astype(BF16)


def pack_rows(layers, low_out, high_out):
    depth, rows, _ = layers.shape
    half = depth // 2
    for d in range(half):
        low_out[d, 0:HALO] = layers[d, 0:HALO]
        low_out[d, HALO : 2 * HALO] = layers[d + half, 0:HALO]
        high_out[d, 0:HALO] = layers[d, rows - HALO : rows]
        high_out[d, HALO : 2 * HALO] = layers[d + half, rows - HALO : rows]


def pack_columns(layers, out):
    depth, rows, columns = layers.shape
    lane = lax.broadcasted_iota(jnp.int32, (rows, columns), 1)
    packed = jnp.zeros((rows, columns), F32)
    for d in range(depth):
        turned = pltpu.roll(layers[d], (2 * HALO * d + HALO) % columns, 1)
        packed = jnp.where(lane // (2 * HALO) == d, turned, packed)
    out[...] = packed


def pack_field(source, field, depth_out, low_out, high_out, column_out):
    depth = source.shape[1]
    depth_out[field, 0:HALO] = source[field, depth - HALO : depth]
    depth_out[field, HALO : 2 * HALO] = source[field, 0:HALO]
    pack_rows(source.at[field], low_out.at[field], high_out.at[field])
    pack_columns(source.at[field], column_out.at[field])


def pack_kernel(
    state_in,
    velocity_in,
    table_in,
    depth_out,
    low_out,
    high_out,
    column_out,
    state,
    velocity,
    table,
    sems,
):
    fields, depth = state.shape[:2]
    outer = depth - HALO
    pairs = [
        (state_in, state),
        (state_in.at[:, outer:depth], depth_out.at[:, 0:HALO]),
        (state_in.at[:, 0:HALO], depth_out.at[:, HALO : 2 * HALO]),
        (velocity_in, velocity),
        (table_in, table),
    ]
    copies = [
        pltpu.make_async_copy(source, target, sems.at[i])
        for i, (source, target) in enumerate(pairs)
    ]
    for copy in copies:
        copy.start()
    copies[0].wait()
    for field in range(fields):
        pack_rows(state.at[field], low_out.at[field], high_out.at[field])
        pack_columns(state.at[field], column_out.at[field])
    for copy in copies[1:]:
        copy.wait()


def reaction(fields, rate):
    rate[...] = (
        RATE_CONST
        * fields[0]
        * fields[1]
        / (1.0 + jnp.exp(-IGNITION_SLOPE * (fields[3] - IGNITION_TEMP)))
    )


def band(cells, targets, columns):
    lane = lax.broadcasted_iota(jnp.int32, cells.shape, 1)
    apart = cells - targets
    distance = jnp.abs(apart)
    first = jnp.zeros(cells.shape, F32)
    second = jnp.zeros(cells.shape, F32)
    for k in range(HALO):
        near = distance == k + 1
        first = jnp.where(near, float(round(FIRST_COEF[k] * FIRST_SCALE)), first)
        second = jnp.where(near, float(round(SECOND_COEF[k] * SECOND_SCALE)), second)
    first = jnp.where(apart < 0, -first, first)
    return jnp.where(lane < columns, first, second).astype(BF16)


def interior_fields(fields, velocity, inner_weight, rate, padded, across, write):
    count, depth, rows, columns = fields.shape
    start = 2 * HALO
    for field in range(count):
        upper, lower = halves(fields[field].reshape(depth * rows, columns))
        across[field] = jnp.dot(
            jnp.concatenate([upper, lower], 1), inner_weight[...], preferred_element_type=F32
        )
        for d in range(depth):
            padded[field, d, start : start + rows] = fields[field, d]
    for field in range(count):
        diffusivity = DIFFUSIVITY[field]
        for d in range(depth):
            centre = fields[field, d]
            laplace = 3.0 * CENTER_COEF * centre
            along_depth = along_row = None
            for k in range(HALO):
                up = padded[field, d, start + k + 1 : start + k + 1 + rows]
                down = padded[field, d, start - k - 1 : start - k - 1 + rows]
                term = FIRST_COEF[k] * (up - down)
                along_row = term if along_row is None else along_row + term
                both = up + down
                ahead = fields[field, d + k + 1] if d + k + 1 < depth else None
                behind = fields[field, d - k - 1] if d - k - 1 >= 0 else None
                if ahead is not None and behind is not None:
                    term = FIRST_COEF[k] * (ahead - behind)
                elif ahead is not None:
                    term = FIRST_COEF[k] * ahead
                else:
                    term = -FIRST_COEF[k] * behind
                along_depth = term if along_depth is None else along_depth + term
                for cells in (ahead, behind):
                    if cells is not None:
                        both = both + cells
                laplace = laplace + SECOND_COEF[k] * both
            here = pl.ds(d * rows, rows)
            along_column = across[field, here, 0:columns]
            laplace = laplace + across[field, here, columns : 2 * columns] * (1.0 / SECOND_SCALE)
            advect = (
                velocity[0, d] * along_depth
                + velocity[1, d] * along_row
                + (velocity[2, d] * (1.0 / FIRST_SCALE)) * along_column
            )
            write(field, d, diffusivity * laplace - advect + SOURCE_COEF[field] * rate[d])


def halo_fields(part, fields, velocity, edge_velocity, halos, halo_weight, scale, write):
    depth_halo, row_below, row_above, column_below, column_above = halos
    low_velocity, high_velocity, column_velocity = edge_velocity
    depth, rows, columns = velocity.shape[1:]
    half = depth // 2
    block = 2 * HALO
    lane = lax.broadcasted_iota(jnp.int32, (rows, columns), 1)
    behind_lane = lane % block < HALO
    edges = jnp.concatenate(
        [jnp.where(behind_lane, column_below[f], column_above[f]) for f in fields], 0
    )
    upper, lower = halves(edges)
    along = jnp.dot(
        jnp.concatenate([upper, lower], 1), halo_weight[...], preferred_element_type=F32
    )
    along_columns = []
    for n, field in enumerate(fields):
        mine = along[n * rows : (n + 1) * rows]
        along_columns.append(
            mine[:, columns:] * (scale * DIFFUSIVITY[field] / SECOND_SCALE)
            - (column_velocity[...] * (scale / FIRST_SCALE)) * mine[:, :columns]
        )

    tile = (block, columns)
    sublane = lax.broadcasted_iota(jnp.int32, tile, 0)
    lane = lax.broadcasted_iota(jnp.int32, tile, 1)
    outer_lane = (lane < HALO) | (lane >= columns - HALO)
    early = sublane < HALO
    step = sublane % HALO
    below_first, below_second, above_first, above_second = [], [], [], []
    for s in range(HALO):
        first, second = FIRST_COEF[HALO - 1 - s], SECOND_COEF[HALO - 1 - s]
        below_first.append(jnp.where(step + s < HALO, -scale * first, 0.0))
        below_second.append(jnp.where(step + s < HALO, scale * second, 0.0))
        above_first.append(jnp.where(step >= s, scale * first, 0.0))
        above_second.append(jnp.where(step >= s, scale * second, 0.0))

    def edge_rows(halo, direction, first_weights, second_weights, speed, diffusivity):
        first = second = None
        for s in range(HALO):
            turned = halo if s == 0 else pltpu.roll(halo, (direction * s) % block, 0)
            one, two = first_weights[s] * turned, second_weights[s] * turned
            first = one if first is None else first + one
            second = two if second is None else second + two
        return diffusivity * second - speed * first

    for n, field in enumerate(fields):
        diffusivity = DIFFUSIVITY[field]
        for i in range(half):
            low = edge_rows(
                row_below[field, i], -1, below_first, below_second, low_velocity[i], diffusivity
            )
            high = edge_rows(
                row_above[field, i], 1, above_first, above_second, high_velocity[i], diffusivity
            )
            for d in (i, i + half):
                low_here = low if d < half else pltpu.roll(low, HALO, 0)
                high_here = pltpu.roll(high, HALO, 0) if d < half else high
                for first_row in range(0, rows, block):
                    here = slice(first_row, first_row + block)
                    value = part[field, d, here]
                    if first_row == 0:
                        value = value + jnp.where(early, low_here, 0.0)
                    if first_row + block == rows:
                        value = value + jnp.where(early, 0.0, high_here)
                    turned = pltpu.roll(
                        along_columns[n][here], (-block * d - HALO) % columns, 1
                    )
                    value = value + jnp.where(outer_lane, turned, 0.0)
                    terms = [(-1, d - k - 1 + HALO, k) for k in range(HALO) if d - k - 1 < 0]
                    terms += [
                        (1, d + k + 1 - depth + HALO, k)
                        for k in range(HALO)
                        if d + k + 1 >= depth
                    ]
                    first = second = None
                    for sign, layer, k in terms:
                        cells = depth_halo[field, layer, here]
                        one = (sign * scale * FIRST_COEF[k]) * cells
                        two = (scale * diffusivity * SECOND_COEF[k]) * cells
                        first = one if first is None else first + one
                        second = two if second is None else second + two
                    if terms:
                        value = value + (second - velocity[0, d, here] * first)
                    write(field, d, here, value)


def first_interior(
    slice_total,
    state,
    velocity,
    table,
    columns_sent,
    part,
    inner_weight,
    halo_weight,
    row_weight,
    column_weight,
    packed_table,
    low_velocity,
    high_velocity,
    column_velocity,
    rate,
    padded,
    across,
):
    del columns_sent
    _, depth, rows, columns = state.shape
    shape = inner_weight.shape
    index = lax.broadcasted_iota(jnp.int32, shape, 0) % columns
    target = lax.broadcasted_iota(jnp.int32, shape, 1) % columns
    inner_weight[...] = band(index, target, columns)
    edge, target_edge = index % (2 * HALO), target % (2 * HALO)
    weight = band(
        jnp.where(edge < HALO, edge, edge + columns) - HALO,
        jnp.where(target_edge < HALO, target_edge + columns, target_edge) - HALO,
        columns,
    )
    same_layer = index // (2 * HALO) == target // (2 * HALO)
    halo_weight[...] = jnp.where(same_layer, weight, jnp.zeros_like(weight))
    pack_rows(velocity.at[1], low_velocity, high_velocity)
    pack_columns(velocity.at[2], column_velocity)
    shape = column_weight.shape
    cell = (lax.broadcasted_iota(jnp.int32, shape, 0) % columns).astype(F32)
    pixel = (lax.broadcasted_iota(jnp.int32, shape, 1) % PIX_C).astype(F32)
    column_weight[...] = tent(pixel, cell, 0.0, columns, PIX_C).astype(BF16)
    half = depth // 2
    place = lax.axis_index("depth") * depth
    shape = (PIX_R, row_weight.shape[2])
    pixel = lax.broadcasted_iota(jnp.int32, shape, 0).astype(F32)
    lane = lax.broadcasted_iota(jnp.int32, shape, 1)
    cell = (lane % rows).astype(F32)
    later = (lane // rows % 2) * half
    for i in range(half):
        level = (place + i + later).astype(F32)
        shift = SHEAR_CELLS * ((level + 0.5) / slice_total - 0.5)
        row_weight[i] = tent(pixel, cell, shift, rows, PIX_R).astype(BF16)
    levels = table.shape[1]
    packed = table[0:1] + table[1:2] * 256 + table[2:3] * 65536 + table[3:4] * 16777216
    packed_table[0:1] = packed
    packed_table[1:2] = jnp.concatenate([packed[:, 1:], packed[:, levels - 1 :]], 1)
    padded[...] = jnp.zeros_like(padded)
    reaction(state, rate)

    def write(field, d, value):
        part[field, d] = state[field, d] + TIME_STEP * value

    interior_fields(state, velocity, inner_weight, rate, padded, across, write)


def first_halo(
    part,
    velocity,
    low_velocity,
    high_velocity,
    column_velocity,
    depth_halo,
    row_below,
    row_above,
    column_below,
    column_above,
    halo_weight,
    middle,
    depth_out,
    low_out,
    high_out,
    column_out,
):
    halos = (depth_halo, row_below, row_above, column_below, column_above)
    edge_velocity = (low_velocity, high_velocity, column_velocity)

    def write(field, d, here, value):
        middle[field, d, here] = value

    fields = range(part.shape[0])
    halo_fields(part, fields, velocity, edge_velocity, halos, halo_weight, TIME_STEP, write)
    for field in fields:
        pack_field(middle, field, depth_out, low_out, high_out, column_out)


def second_interior(
    middle, state, velocity, inner_weight, columns_sent, part, rate, padded, across
):
    del columns_sent
    padded[...] = jnp.zeros_like(padded)
    reaction(middle, rate)

    def write(field, d, value):
        part[field, d] = 0.5 * (state[field, d] + middle[field, d]) + (0.5 * TIME_STEP) * value

    interior_fields(middle, velocity, inner_weight, rate, padded, across, write)


def tent(pixel, cell, shift, cells, pixels):
    stride = cells / pixels
    reach = max(1.0, stride)
    at = jnp.clip((pixel + 0.5) * stride - 0.5 + shift, 0.0, cells - 1.0)
    return jnp.maximum(0.0, 1.0 - jnp.abs(at - cell) / reach) / reach


def sample_slices(temperature, column_weight, row_weight, samples):
    depth, rows, columns = temperature.shape
    half = depth // 2
    upper, lower = halves(temperature[...].reshape(depth * rows, columns))
    wide = jnp.dot(
        jnp.concatenate([upper, lower], 1), column_weight[...], preferred_element_type=F32
    )
    lane = lax.broadcasted_iota(jnp.int32, (rows, 2 * PIX_C), 1)
    for i in range(half):
        left = jnp.where(lane < PIX_C, wide[i * rows : (i + 1) * rows], 0.0)
        right = jnp.where(
            lane < PIX_C, 0.0, wide[(i + half) * rows : (i + half + 1) * rows]
        )
        both_upper, both_lower = halves(jnp.concatenate([left, right], 0))
        samples[i] = jnp.dot(
            row_weight[i],
            jnp.concatenate([both_upper, both_lower], 0),
            preferred_element_type=F32,
        )


def look_up(tables, index, shape):
    lanes = tables[0].shape[1]
    inside = index & (lanes - 1)
    result = None
    for part, table in enumerate(tables):
        found = jnp.take_along_axis(
            jnp.broadcast_to(table, shape), inside, axis=1, mode="promise_in_bounds"
        )
        result = found if part == 0 else jnp.where(index >= part * lanes, found, result)
    return result


def march(samples, table, flag, slice_total, share):
    half, pixel_rows, lanes = samples.shape
    levels = table.shape[1]
    below_tables = [table[0:1, i : i + lanes] for i in range(0, levels, lanes)]
    above_tables = [table[1:2, i : i + lanes] for i in range(0, levels, lanes)]
    shape = (pixel_rows // 2, lanes)
    lane = lax.broadcasted_iota(jnp.int32, shape, 1)
    in_front = (lane < PIX_C) == (flag == 0)
    parts = []
    for part in range(2):
        rows_here = pl.ds(part * shape[0], shape[0])

        def advance(position, running):
            chosen = jnp.where(flag == 0, half - 1 - position, position)
            level = jnp.clip(samples[chosen, rows_here] * (levels - 1.0), 0.0, levels - 1.0)
            lower = level.astype(jnp.int32)
            fraction = level - lower.astype(F32)
            below = look_up(below_tables, lower, shape)
            above = look_up(above_tables, lower, shape)
            raw = []
            for channel in range(4):
                low, high = below, above
                if channel > 0:
                    low = lax.shift_right_logical(low, 8 * channel)
                    high = lax.shift_right_logical(high, 8 * channel)
                if channel < 3:
                    low, high = low & 255, high & 255
                low, high = low.astype(F32), high.astype(F32)
                raw.append(low + fraction * (high - low))
            alpha = raw[3] * (OPACITY_TOTAL / slice_total / 255.0)
            through = 1.0 - alpha
            return tuple(
                [alpha * raw[c] + through * running[c] for c in range(3)]
                + [alpha + through * running[3]]
            )

        zero = jnp.zeros(shape, F32)
        running = lax.fori_loop(0, half, advance, (zero, zero, zero, zero), unroll=True)
        parts.append([value * (1.0 / 255.0) for value in running[:3]] + [running[3]])
    for channel in range(4):
        merged = []
        for part in range(2):
            own, own_alpha = parts[part][channel], parts[part][3]
            other, other_alpha = pltpu.roll(own, PIX_C, 1), pltpu.roll(own_alpha, PIX_C, 1)
            merged.append(
                jnp.where(
                    in_front, own + (1.0 - own_alpha) * other, other + (1.0 - other_alpha) * own
                )
            )
        share[channel] = jnp.where(lane < PIX_C, merged[0], merged[1])


def temperature_halo(
    slice_total,
    order,
    part,
    velocity,
    low_velocity,
    high_velocity,
    column_velocity,
    depth_halo,
    row_below,
    row_above,
    column_below,
    column_above,
    halo_weight,
    column_weight,
    row_weight,
    table,
    temperature,
    share,
    toward,
    samples,
):
    halos = (depth_halo, row_below, row_above, column_below, column_above)
    edge_velocity = (low_velocity, high_velocity, column_velocity)

    def write(field, d, here, value):
        temperature[d, here] = value

    halo_fields(part, [3], velocity, edge_velocity, halos, halo_weight, 0.5 * TIME_STEP, write)
    sample_slices(temperature, column_weight, row_weight, samples)
    toward[...] = jnp.full(toward.shape, order[0, 0], jnp.int32)
    march(samples, table, order[0, 0], slice_total, share)


def fractions_halo(
    part,
    temperature,
    velocity,
    low_velocity,
    high_velocity,
    column_velocity,
    depth_halo,
    row_below,
    row_above,
    column_below,
    column_above,
    halo_weight,
    share,
    new_state,
):
    del share
    halos = (depth_halo, row_below, row_above, column_below, column_above)
    edge_velocity = (low_velocity, high_velocity, column_velocity)

    def write(field, d, here, value):
        new_state[field, d, here] = value

    halo_fields(
        part, range(3), velocity, edge_velocity, halos, halo_weight, 0.5 * TIME_STEP, write
    )
    new_state[3] = temperature[...]


def merge_kernel(bit, last, toward, own, received, out):
    shape = own.shape[1:]
    mine = lax.axis_index("depth") // 2**bit % 2
    front = jnp.broadcast_to(toward[0:1] == mine, shape)
    own_alpha, received_alpha = own[3], received[3]
    for channel in range(4):
        one, two = own[channel], received[channel]
        front_value = one + (1.0 - own_alpha) * two
        back_value = two + (1.0 - received_alpha) * one
        value = jnp.where(front, front_value, back_value)
        if last:
            out[channel, 0 : shape[0]] = value[:, 0:PIX_C]
            out[channel, shape[0] : 2 * shape[0]] = pltpu.roll(value, PIX_C, 1)[:, 0:PIX_C]
        else:
            out[channel] = value


def shift(value, axis, step):
    count = lax.axis_size(axis)
    return lax.ppermute(value, axis, [(i, (i + step) % count) for i in range(count)])


def exchange(depth_faces, low_rows, high_rows, columns):
    if lax.axis_size("depth") == 2:
        depth_halo = shift(depth_faces, "depth", 1)
    else:
        depth_halo = jnp.concatenate(
            [
                shift(depth_faces[:, :HALO], "depth", 1),
                shift(depth_faces[:, HALO:], "depth", -1),
            ],
            1,
        )
    row_below = shift(high_rows, "row", 1)
    row_above = shift(low_rows, "row", -1)
    column_below = shift(columns, "col", 1)
    column_above = shift(columns, "col", -1)
    return depth_halo, row_below, row_above, column_below, column_above


def call(kernel, outs, scratch, specs, *args):
    vmem = pl.BlockSpec(memory_space=pltpu.VMEM)
    return pl.pallas_call(
        kernel,
        out_shape=outs,
        in_specs=specs + [vmem] * (len(args) - len(specs)),
        out_specs=jax.tree.map(lambda _: vmem, outs),
        scratch_shapes=scratch,
        compiler_params=pltpu.CompilerParams(vmem_limit_bytes=VMEM_LIMIT),
    )(*args)


def in_hbm(value):
    return pltpu.with_memory_space_constraint(value, pltpu.HBM)


def local(state, velocity, view_order, tf_table):
    fields, depth, rows, columns = state.shape
    depth_count = lax.axis_size("depth")

    def array(*shape, dtype=F32):
        return jax.ShapeDtypeStruct(shape, dtype)

    whole = array(*state.shape)
    faces = (
        array(fields, 2 * HALO, rows, columns),
        array(fields, depth // 2, 2 * HALO, columns),
        array(fields, depth // 2, 2 * HALO, columns),
        array(fields, rows, columns),
    )
    inner_work = [
        pltpu.VMEM((depth, rows, columns), F32),
        pltpu.VMEM((fields, depth, rows + 4 * HALO, columns), F32),
        pltpu.VMEM((fields, depth * rows, 2 * columns), F32),
    ]
    edge_rows = array(depth // 2, 2 * HALO, columns)
    slice_total = depth * depth_count

    hbm = pl.BlockSpec(memory_space=pltpu.HBM)
    *sent, state, velocity, table = call(
        pack_kernel,
        faces + (whole, array(*velocity.shape), array(*tf_table.shape, dtype=jnp.int32)),
        [pltpu.SemaphoreType.DMA((5,))],
        [hbm, hbm, hbm],
        in_hbm(state),
        in_hbm(velocity),
        in_hbm(tf_table),
    )
    halos = exchange(*sent)
    part, inner_weight, halo_weight, row_weight, column_weight, table, *edge_velocity = call(
        functools.partial(first_interior, slice_total),
        (
            whole,
            array(2 * columns, 2 * columns, dtype=BF16),
            array(2 * columns, 2 * columns, dtype=BF16),
            array(depth // 2, PIX_R, 4 * rows, dtype=BF16),
            array(2 * columns, 2 * PIX_C, dtype=BF16),
            array(2, tf_table.shape[1], dtype=jnp.int32),
            edge_rows,
            edge_rows,
            array(rows, columns),
        ),
        inner_work,
        [],
        state,
        velocity,
        table,
        sent[3],
    )
    middle, *sent = call(
        first_halo,
        (whole,) + faces,
        [],
        [],
        part,
        velocity,
        *edge_velocity,
        *halos,
        halo_weight,
    )
    halos = exchange(*sent)
    part = call(
        second_interior,
        whole,
        inner_work,
        [],
        middle,
        state,
        velocity,
        inner_weight,
        sent[3],
    )
    temperature, share, toward = call(
        functools.partial(temperature_halo, slice_total),
        (
            array(depth, rows, columns),
            array(4, PIX_R // 2, 2 * PIX_C),
            array(8, 2 * PIX_C, dtype=jnp.int32),
        ),
        [pltpu.VMEM((depth // 2, PIX_R, 2 * PIX_C), F32)],
        [pl.BlockSpec(memory_space=pltpu.SMEM)],
        view_order,
        part,
        velocity,
        *edge_velocity,
        *halos,
        halo_weight,
        column_weight,
        row_weight,
        table,
    )
    new_state = call(
        fractions_halo,
        whole,
        [],
        [],
        part,
        temperature,
        velocity,
        *edge_velocity,
        *halos,
        halo_weight,
        share,
    )
    bits = depth_count.bit_length() - 1
    for bit in range(bits):
        pairs = [(i, i ^ 2**bit) for i in range(depth_count)]
        received = lax.ppermute(share, "depth", pairs)
        last = bit == bits - 1
        share = call(
            functools.partial(merge_kernel, bit, last),
            array(4, PIX_R, PIX_C) if last else array(*share.shape),
            [],
            [],
            toward,
            share,
            received,
        )
    return new_state, share


def solution(mesh):
    in_specs = (
        P(None, "depth", "row", "col"),
        P(None, "depth", "row", "col"),
        P("row", "col"),
        P(),
    )
    out_specs = (P(None, "depth", "row", "col"), P(None, "row", "col"))
    return jax.shard_map(local, mesh=mesh, in_specs=in_specs, out_specs=out_specs, check_vma=False)
```

```python
import functools

import jax
import jax.numpy as jnp
from jax import lax
from jax.experimental import pallas as pl
from jax.experimental.pallas import tpu as pltpu
from jax.sharding import PartitionSpec as P

PIX_R = 64
PIX_C = 64
HALO = 4

FIRST_COEF = (0.8, -0.2, 4.0 / 105.0, -1.0 / 280.0)
SECOND_COEF = (1.6, -0.2, 8.0 / 315.0, -1.0 / 560.0)
CENTER_COEF = -205.0 / 72.0
FIRST_SCALE = 840
SECOND_SCALE = 5040
DIFFUSIVITY = (0.05, 0.04, 0.03, 0.08)
TIME_STEP = 0.2
RATE_CONST = 2.0
IGNITION_SLOPE = 8.0
IGNITION_TEMP = 0.5
OXIDIZER_RATIO = 1.5
HEAT_RELEASE = 0.8
SHEAR_CELLS = 2.0
OPACITY_TOTAL = 6.0
SOURCE_COEF = (-1.0, -OXIDIZER_RATIO, 1.0 + OXIDIZER_RATIO, HEAT_RELEASE)

VMEM_LIMIT = 24 * 1024 * 1024
F32 = jnp.float32
BF16 = jnp.bfloat16


def halves(value):
    upper = value.astype(BF16)
    return upper, (value - upper.astype(F32)).astype(BF16)


def pack_rows(layers, low_out, high_out):
    depth, rows, _ = layers.shape
    half = depth // 2
    for d in range(half):
        low_out[d, 0:HALO] = layers[d, 0:HALO]
        low_out[d, HALO : 2 * HALO] = layers[d + half, 0:HALO]
        high_out[d, 0:HALO] = layers[d, rows - HALO : rows]
        high_out[d, HALO : 2 * HALO] = layers[d + half, rows - HALO : rows]


def pack_columns(layers, out):
    depth, rows, columns = layers.shape
    lane = lax.broadcasted_iota(jnp.int32, (rows, columns), 1)
    packed = jnp.zeros((rows, columns), F32)
    for d in range(depth):
        turned = pltpu.roll(layers[d], (2 * HALO * d + HALO) % columns, 1)
        packed = jnp.where(lane // (2 * HALO) == d, turned, packed)
    out[...] = packed


def pack_field(source, field, depth_out, low_out, high_out, column_out):
    depth = source.shape[1]
    depth_out[field, 0:HALO] = source[field, depth - HALO : depth]
    depth_out[field, HALO : 2 * HALO] = source[field, 0:HALO]
    pack_rows(source.at[field], low_out.at[field], high_out.at[field])
    pack_columns(source.at[field], column_out.at[field])


def pack_kernel(
    state_in,
    velocity_in,
    table_in,
    depth_out,
    low_out,
    high_out,
    column_out,
    state,
    velocity,
    table,
    sems,
):
    fields, depth = state.shape[:2]
    outer = depth - HALO
    pairs = [
        (state_in, state),
        (state_in.at[:, outer:depth], depth_out.at[:, 0:HALO]),
        (state_in.at[:, 0:HALO], depth_out.at[:, HALO : 2 * HALO]),
        (velocity_in, velocity),
        (table_in, table),
    ]
    copies = [
        pltpu.make_async_copy(source, target, sems.at[i])
        for i, (source, target) in enumerate(pairs)
    ]
    for copy in copies:
        copy.start()
    copies[0].wait()
    for field in range(fields):
        pack_rows(state.at[field], low_out.at[field], high_out.at[field])
        pack_columns(state.at[field], column_out.at[field])
    for copy in copies[1:]:
        copy.wait()


def reaction(fields, rate):
    rate[...] = (
        RATE_CONST
        * fields[0]
        * fields[1]
        / (1.0 + jnp.exp(-IGNITION_SLOPE * (fields[3] - IGNITION_TEMP)))
    )


def band(cells, targets, columns):
    lane = lax.broadcasted_iota(jnp.int32, cells.shape, 1)
    apart = cells - targets
    distance = jnp.abs(apart)
    first = jnp.zeros(cells.shape, F32)
    second = jnp.zeros(cells.shape, F32)
    for k in range(HALO):
        near = distance == k + 1
        first = jnp.where(near, float(round(FIRST_COEF[k] * FIRST_SCALE)), first)
        second = jnp.where(near, float(round(SECOND_COEF[k] * SECOND_SCALE)), second)
    first = jnp.where(apart < 0, -first, first)
    return jnp.where(lane < columns, first, second).astype(BF16)


def interior_fields(fields, velocity, inner_weight, rate, padded, across, write):
    count, depth, rows, columns = fields.shape
    start = 2 * HALO
    for field in range(count):
        upper, lower = halves(fields[field].reshape(depth * rows, columns))
        across[field] = jnp.dot(
            jnp.concatenate([upper, lower], 1), inner_weight[...], preferred_element_type=F32
        )
        for d in range(depth):
            padded[field, d, start : start + rows] = fields[field, d]
    for field in range(count):
        diffusivity = DIFFUSIVITY[field]
        for d in range(depth):
            centre = fields[field, d]
            laplace = 3.0 * CENTER_COEF * centre
            along_depth = along_row = None
            for k in range(HALO):
                up = padded[field, d, start + k + 1 : start + k + 1 + rows]
                down = padded[field, d, start - k - 1 : start - k - 1 + rows]
                term = FIRST_COEF[k] * (up - down)
                along_row = term if along_row is None else along_row + term
                both = up + down
                ahead = fields[field, d + k + 1] if d + k + 1 < depth else None
                behind = fields[field, d - k - 1] if d - k - 1 >= 0 else None
                if ahead is not None and behind is not None:
                    term = FIRST_COEF[k] * (ahead - behind)
                elif ahead is not None:
                    term = FIRST_COEF[k] * ahead
                else:
                    term = -FIRST_COEF[k] * behind
                along_depth = term if along_depth is None else along_depth + term
                for cells in (ahead, behind):
                    if cells is not None:
                        both = both + cells
                laplace = laplace + SECOND_COEF[k] * both
            here = pl.ds(d * rows, rows)
            along_column = across[field, here, 0:columns]
            laplace = laplace + across[field, here, columns : 2 * columns] * (1.0 / SECOND_SCALE)
            advect = (
                velocity[0, d] * along_depth
                + velocity[1, d] * along_row
                + (velocity[2, d] * (1.0 / FIRST_SCALE)) * along_column
            )
            write(field, d, diffusivity * laplace - advect + SOURCE_COEF[field] * rate[d])


def halo_fields(part, fields, velocity, edge_velocity, halos, halo_weight, scale, write):
    depth_halo, row_above, row_below, column_below, column_above = halos
    low_velocity, high_velocity, column_velocity = edge_velocity
    depth, rows, columns = velocity.shape[1:]
    half = depth // 2
    block = 2 * HALO
    lane = lax.broadcasted_iota(jnp.int32, (rows, columns), 1)
    behind_lane = lane % block < HALO
    edges = jnp.concatenate(
        [jnp.where(behind_lane, column_below[f], column_above[f]) for f in fields], 0
    )
    upper, lower = halves(edges)
    along = jnp.dot(
        jnp.concatenate([upper, lower], 1), halo_weight[...], preferred_element_type=F32
    )
    along_columns = []
    for n, field in enumerate(fields):
        mine = along[n * rows : (n + 1) * rows]
        along_columns.append(
            mine[:, columns:] * (scale * DIFFUSIVITY[field] / SECOND_SCALE)
            - (column_velocity[...] * (scale / FIRST_SCALE)) * mine[:, :columns]
        )

    tile = (block, columns)
    sublane = lax.broadcasted_iota(jnp.int32, tile, 0)
    lane = lax.broadcasted_iota(jnp.int32, tile, 1)
    outer_lane = (lane < HALO) | (lane >= columns - HALO)
    early = sublane < HALO
    step = sublane % HALO
    below_first, below_second, above_first, above_second = [], [], [], []
    for s in range(HALO):
        first, second = FIRST_COEF[HALO - 1 - s], SECOND_COEF[HALO - 1 - s]
        below_first.append(jnp.where(step + s < HALO, -scale * first, 0.0))
        below_second.append(jnp.where(step + s < HALO, scale * second, 0.0))
        above_first.append(jnp.where(step >= s, scale * first, 0.0))
        above_second.append(jnp.where(step >= s, scale * second, 0.0))

    def edge_rows(halo, direction, first_weights, second_weights, speed, diffusivity):
        first = second = None
        for s in range(HALO):
            turned = halo if s == 0 else pltpu.roll(halo, (direction * s) % block, 0)
            one, two = first_weights[s] * turned, second_weights[s] * turned
            first = one if first is None else first + one
            second = two if second is None else second + two
        return diffusivity * second - speed * first

    for n, field in enumerate(fields):
        diffusivity = DIFFUSIVITY[field]
        for i in range(half):
            low = edge_rows(
                row_below[field, i], -1, below_first, below_second, low_velocity[i], diffusivity
            )
            high = edge_rows(
                row_above[field, i], 1, above_first, above_second, high_velocity[i], diffusivity
            )
            for d in (i, i + half):
                low_here = low if d < half else pltpu.roll(low, HALO, 0)
                high_here = pltpu.roll(high, HALO, 0) if d < half else high
                for first_row in range(0, rows, block):
                    here = slice(first_row, first_row + block)
                    value = part[field, d, here]
                    if first_row == 0:
                        value = value + jnp.where(early, low_here, 0.0)
                    if first_row + block == rows:
                        value = value + jnp.where(early, 0.0, high_here)
                    turned = pltpu.roll(
                        along_columns[n][here], (-block * d - HALO) % columns, 1
                    )
                    value = value + jnp.where(outer_lane, turned, 0.0)
                    terms = [(-1, d - k - 1 + HALO, k) for k in range(HALO) if d - k - 1 < 0]
                    terms += [
                        (1, d + k + 1 - depth + HALO, k)
                        for k in range(HALO)
                        if d + k + 1 >= depth
                    ]
                    first = second = None
                    for sign, layer, k in terms:
                        cells = depth_halo[field, layer, here]
                        one = (sign * scale * FIRST_COEF[k]) * cells
                        two = (scale * diffusivity * SECOND_COEF[k]) * cells
                        first = one if first is None else first + one
                        second = two if second is None else second + two
                    if terms:
                        value = value + (second - velocity[0, d, here] * first)
                    write(field, d, here, value)


def first_interior(
    slice_total,
    state,
    velocity,
    table,
    columns_sent,
    part,
    inner_weight,
    halo_weight,
    row_weight,
    column_weight,
    packed_table,
    low_velocity,
    high_velocity,
    column_velocity,
    rate,
    padded,
    across,
):
    del columns_sent
    _, depth, rows, columns = state.shape
    shape = inner_weight.shape
    index = lax.broadcasted_iota(jnp.int32, shape, 0) % columns
    target = lax.broadcasted_iota(jnp.int32, shape, 1) % columns
    inner_weight[...] = band(index, target, columns)
    edge, target_edge = index % (2 * HALO), target % (2 * HALO)
    weight = band(
        jnp.where(edge < HALO, edge, edge + columns) - HALO,
        jnp.where(target_edge < HALO, target_edge + columns, target_edge) - HALO,
        columns,
    )
    same_layer = index // (2 * HALO) == target // (2 * HALO)
    halo_weight[...] = jnp.where(same_layer, weight, jnp.zeros_like(weight))
    pack_rows(velocity.at[1], low_velocity, high_velocity)
    pack_columns(velocity.at[2], column_velocity)
    shape = column_weight.shape
    cell = (lax.broadcasted_iota(jnp.int32, shape, 0) % columns).astype(F32)
    pixel = (lax.broadcasted_iota(jnp.int32, shape, 1) % PIX_C).astype(F32)
    column_weight[...] = tent(pixel, cell, 0.0, columns, PIX_C).astype(BF16)
    half = depth // 2
    place = lax.axis_index("depth") * depth
    shape = (PIX_R, row_weight.shape[2])
    pixel = lax.broadcasted_iota(jnp.int32, shape, 0).astype(F32)
    lane = lax.broadcasted_iota(jnp.int32, shape, 1)
    cell = (lane % rows).astype(F32)
    later = (lane // rows % 2) * half
    for i in range(half):
        level = (place + i + later).astype(F32)
        shift = SHEAR_CELLS * ((level + 0.5) / slice_total - 0.5)
        row_weight[i] = tent(pixel, cell, shift, rows, PIX_R).astype(BF16)
    levels = table.shape[1]
    packed = table[0:1] + table[1:2] * 256 + table[2:3] * 65536 + table[3:4] * 16777216
    packed_table[0:1] = packed
    packed_table[1:2] = jnp.concatenate([packed[:, 1:], packed[:, levels - 1 :]], 1)
    padded[...] = jnp.zeros_like(padded)
    reaction(state, rate)

    def write(field, d, value):
        part[field, d] = state[field, d] + TIME_STEP * value

    interior_fields(state, velocity, inner_weight, rate, padded, across, write)


def first_halo(
    part,
    velocity,
    low_velocity,
    high_velocity,
    column_velocity,
    depth_halo,
    row_above,
    row_below,
    column_below,
    column_above,
    halo_weight,
    middle,
    depth_out,
    low_out,
    high_out,
    column_out,
):
    halos = (depth_halo, row_above, row_below, column_below, column_above)
    edge_velocity = (low_velocity, high_velocity, column_velocity)

    def write(field, d, here, value):
        middle[field, d, here] = value

    fields = range(part.shape[0])
    halo_fields(part, fields, velocity, edge_velocity, halos, halo_weight, TIME_STEP, write)
    for field in fields:
        pack_field(middle, field, depth_out, low_out, high_out, column_out)


def second_interior(
    middle, state, velocity, inner_weight, columns_sent, part, rate, padded, across
):
    del columns_sent
    padded[...] = jnp.zeros_like(padded)
    reaction(middle, rate)

    def write(field, d, value):
        part[field, d] = 0.5 * (state[field, d] + middle[field, d]) + (0.5 * TIME_STEP) * value

    interior_fields(middle, velocity, inner_weight, rate, padded, across, write)


def tent(pixel, cell, shift, cells, pixels):
    stride = cells / pixels
    reach = max(1.0, stride)
    at = jnp.clip((pixel + 0.5) * stride - 0.5 + shift, 0.0, cells - 1.0)
    return jnp.maximum(0.0, 1.0 - jnp.abs(at - cell) / reach) / reach


def sample_slices(temperature, column_weight, row_weight, samples):
    depth, rows, columns = temperature.shape
    half = depth // 2
    upper, lower = halves(temperature[...].reshape(depth * rows, columns))
    wide = jnp.dot(
        jnp.concatenate([upper, lower], 1), column_weight[...], preferred_element_type=F32
    )
    lane = lax.broadcasted_iota(jnp.int32, (rows, 2 * PIX_C), 1)
    for i in range(half):
        left = jnp.where(lane < PIX_C, wide[i * rows : (i + 1) * rows], 0.0)
        right = jnp.where(
            lane < PIX_C, 0.0, wide[(i + half) * rows : (i + half + 1) * rows]
        )
        both_upper, both_lower = halves(jnp.concatenate([left, right], 0))
        samples[i] = jnp.dot(
            row_weight[i],
            jnp.concatenate([both_upper, both_lower], 0),
            preferred_element_type=F32,
        )


def look_up(tables, index, shape):
    lanes = tables[0].shape[1]
    inside = index & (lanes - 1)
    result = None
    for part, table in enumerate(tables):
        found = jnp.take_along_axis(
            jnp.broadcast_to(table, shape), inside, axis=1, mode="promise_in_bounds"
        )
        result = found if part == 0 else jnp.where(index >= part * lanes, found, result)
    return result


def march(samples, table, flag, slice_total, share):
    half, pixel_rows, lanes = samples.shape
    levels = table.shape[1]
    below_tables = [table[0:1, i : i + lanes] for i in range(0, levels, lanes)]
    above_tables = [table[1:2, i : i + lanes] for i in range(0, levels, lanes)]
    shape = (pixel_rows // 2, lanes)
    lane = lax.broadcasted_iota(jnp.int32, shape, 1)
    in_front = (lane < PIX_C) == (flag == 0)
    parts = []
    for part in range(2):
        rows_here = pl.ds(part * shape[0], shape[0])

        def advance(position, running):
            chosen = jnp.where(flag == 0, half - 1 - position, position)
            level = jnp.clip(samples[chosen, rows_here] * (levels - 1.0), 0.0, levels - 1.0)
            lower = level.astype(jnp.int32)
            fraction = level - lower.astype(F32)
            below = look_up(below_tables, lower, shape)
            above = look_up(above_tables, lower, shape)
            raw = []
            for channel in range(4):
                low, high = below, above
                if channel > 0:
                    low = lax.shift_right_logical(low, 8 * channel)
                    high = lax.shift_right_logical(high, 8 * channel)
                if channel < 3:
                    low, high = low & 255, high & 255
                low, high = low.astype(F32), high.astype(F32)
                raw.append(low + fraction * (high - low))
            alpha = raw[3] * (OPACITY_TOTAL / slice_total / 255.0)
            through = 1.0 - alpha
            return tuple(
                [alpha * raw[c] + through * running[c] for c in range(3)]
                + [alpha + through * running[3]]
            )

        zero = jnp.zeros(shape, F32)
        running = lax.fori_loop(0, half, advance, (zero, zero, zero, zero), unroll=True)
        parts.append([value * (1.0 / 255.0) for value in running[:3]] + [running[3]])
    for channel in range(4):
        merged = []
        for part in range(2):
            own, own_alpha = parts[part][channel], parts[part][3]
            other, other_alpha = pltpu.roll(own, PIX_C, 1), pltpu.roll(own_alpha, PIX_C, 1)
            merged.append(
                jnp.where(
                    in_front, own + (1.0 - own_alpha) * other, other + (1.0 - other_alpha) * own
                )
            )
        share[channel] = jnp.where(lane < PIX_C, merged[0], merged[1])


def temperature_halo(
    slice_total,
    order,
    part,
    velocity,
    low_velocity,
    high_velocity,
    column_velocity,
    depth_halo,
    row_above,
    row_below,
    column_below,
    column_above,
    halo_weight,
    column_weight,
    row_weight,
    table,
    temperature,
    share,
    toward,
    samples,
):
    halos = (depth_halo, row_above, row_below, column_below, column_above)
    edge_velocity = (low_velocity, high_velocity, column_velocity)

    def write(field, d, here, value):
        temperature[d, here] = value

    halo_fields(part, [3], velocity, edge_velocity, halos, halo_weight, 0.5 * TIME_STEP, write)
    sample_slices(temperature, column_weight, row_weight, samples)
    toward[...] = jnp.full(toward.shape, order[0, 0], jnp.int32)
    march(samples, table, order[0, 0], slice_total, share)


def fractions_halo(
    part,
    temperature,
    velocity,
    low_velocity,
    high_velocity,
    column_velocity,
    depth_halo,
    row_above,
    row_below,
    column_below,
    column_above,
    halo_weight,
    share,
    new_state,
):
    del share
    halos = (depth_halo, row_above, row_below, column_below, column_above)
    edge_velocity = (low_velocity, high_velocity, column_velocity)

    def write(field, d, here, value):
        new_state[field, d, here] = value

    halo_fields(
        part, range(3), velocity, edge_velocity, halos, halo_weight, 0.5 * TIME_STEP, write
    )
    new_state[3] = temperature[...]


def merge_kernel(bit, last, toward, own, received, out):
    shape = own.shape[1:]
    mine = lax.axis_index("depth") // 2**bit % 2
    front = jnp.broadcast_to(toward[0:1] == mine, shape)
    own_alpha, received_alpha = own[3], received[3]
    for channel in range(4):
        one, two = own[channel], received[channel]
        front_value = one + (1.0 - own_alpha) * two
        back_value = two + (1.0 - received_alpha) * one
        value = jnp.where(front, front_value, back_value)
        if last:
            out[channel, 0 : shape[0]] = value[:, 0:PIX_C]
            out[channel, shape[0] : 2 * shape[0]] = pltpu.roll(value, PIX_C, 1)[:, 0:PIX_C]
        else:
            out[channel] = value


def shift(value, axis, step):
    count = lax.axis_size(axis)
    return lax.ppermute(value, axis, [(i, (i + step) % count) for i in range(count)])


def exchange(depth_faces, low_rows, high_rows, columns):
    if lax.axis_size("depth") == 2:
        depth_halo = shift(depth_faces, "depth", 1)
    else:
        depth_halo = jnp.concatenate(
            [
                shift(depth_faces[:, :HALO], "depth", 1),
                shift(depth_faces[:, HALO:], "depth", -1),
            ],
            1,
        )
    row_below = shift(high_rows, "row", 1)
    row_above = shift(low_rows, "row", -1)
    column_below = shift(columns, "col", 1)
    column_above = shift(columns, "col", -1)
    return depth_halo, row_above, row_below, column_below, column_above


def call(kernel, outs, scratch, specs, *args):
    vmem = pl.BlockSpec(memory_space=pltpu.VMEM)
    return pl.pallas_call(
        kernel,
        out_shape=outs,
        in_specs=specs + [vmem] * (len(args) - len(specs)),
        out_specs=jax.tree.map(lambda _: vmem, outs),
        scratch_shapes=scratch,
        compiler_params=pltpu.CompilerParams(vmem_limit_bytes=VMEM_LIMIT),
    )(*args)


def in_hbm(value):
    return pltpu.with_memory_space_constraint(value, pltpu.HBM)


def local(state, velocity, view_order, tf_table):
    fields, depth, rows, columns = state.shape
    depth_count = lax.axis_size("depth")

    def array(*shape, dtype=F32):
        return jax.ShapeDtypeStruct(shape, dtype)

    whole = array(*state.shape)
    faces = (
        array(fields, 2 * HALO, rows, columns),
        array(fields, depth // 2, 2 * HALO, columns),
        array(fields, depth // 2, 2 * HALO, columns),
        array(fields, rows, columns),
    )
    inner_work = [
        pltpu.VMEM((depth, rows, columns), F32),
        pltpu.VMEM((fields, depth, rows + 4 * HALO, columns), F32),
        pltpu.VMEM((fields, depth * rows, 2 * columns), F32),
    ]
    edge_rows = array(depth // 2, 2 * HALO, columns)
    slice_total = depth * depth_count

    hbm = pl.BlockSpec(memory_space=pltpu.HBM)
    *sent, state, velocity, table = call(
        pack_kernel,
        faces + (whole, array(*velocity.shape), array(*tf_table.shape, dtype=jnp.int32)),
        [pltpu.SemaphoreType.DMA((5,))],
        [hbm, hbm, hbm],
        in_hbm(state),
        in_hbm(velocity),
        in_hbm(tf_table),
    )
    halos = exchange(*sent)
    part, inner_weight, halo_weight, row_weight, column_weight, table, *edge_velocity = call(
        functools.partial(first_interior, slice_total),
        (
            whole,
            array(2 * columns, 2 * columns, dtype=BF16),
            array(2 * columns, 2 * columns, dtype=BF16),
            array(depth // 2, PIX_R, 4 * rows, dtype=BF16),
            array(2 * columns, 2 * PIX_C, dtype=BF16),
            array(2, tf_table.shape[1], dtype=jnp.int32),
            edge_rows,
            edge_rows,
            array(rows, columns),
        ),
        inner_work,
        [],
        state,
        velocity,
        table,
        sent[3],
    )
    middle, *sent = call(
        first_halo,
        (whole,) + faces,
        [],
        [],
        part,
        velocity,
        *edge_velocity,
        *halos,
        halo_weight,
    )
    halos = exchange(*sent)
    part = call(
        second_interior,
        whole,
        inner_work,
        [],
        middle,
        state,
        velocity,
        inner_weight,
        sent[3],
    )
    temperature, share, toward = call(
        functools.partial(temperature_halo, slice_total),
        (
            array(depth, rows, columns),
            array(4, PIX_R // 2, 2 * PIX_C),
            array(8, 2 * PIX_C, dtype=jnp.int32),
        ),
        [pltpu.VMEM((depth // 2, PIX_R, 2 * PIX_C), F32)],
        [pl.BlockSpec(memory_space=pltpu.SMEM)],
        view_order,
        part,
        velocity,
        *edge_velocity,
        *halos,
        halo_weight,
        column_weight,
        row_weight,
        table,
    )
    new_state = call(
        fractions_halo,
        whole,
        [],
        [],
        part,
        temperature,
        velocity,
        *edge_velocity,
        *halos,
        halo_weight,
        share,
    )
    bits = depth_count.bit_length() - 1
    for bit in range(bits):
        pairs = [(i, i ^ 2**bit) for i in range(depth_count)]
        received = lax.ppermute(share, "depth", pairs)
        last = bit == bits - 1
        share = call(
            functools.partial(merge_kernel, bit, last),
            array(4, PIX_R, PIX_C) if last else array(*share.shape),
            [],
            [],
            toward,
            share,
            received,
        )
    return new_state, share


def solution(mesh):
    in_specs = (
        P(None, "depth", "row", "col"),
        P(None, "depth", "row", "col"),
        P("row", "col"),
        P(),
    )
    out_specs = (P(None, "depth", "row", "col"), P(None, "row", "col"))
    return jax.shard_map(local, mesh=mesh, in_specs=in_specs, out_specs=out_specs, check_vma=False)
```

```python
import functools

import jax
import jax.numpy as jnp
from jax import lax
from jax.experimental import pallas as pl
from jax.experimental.pallas import tpu as pltpu
from jax.sharding import PartitionSpec as P

PIX_R = 64
PIX_C = 64
HALO = 4

FIRST_COEF = (0.8, -0.2, 4.0 / 105.0, -1.0 / 280.0)
SECOND_COEF = (1.6, -0.2, 8.0 / 315.0, -1.0 / 560.0)
CENTER_COEF = -205.0 / 72.0
FIRST_SCALE = 840
SECOND_SCALE = 5040
DIFFUSIVITY = (0.05, 0.04, 0.03, 0.08)
TIME_STEP = 0.2
RATE_CONST = 2.0
IGNITION_SLOPE = 8.0
IGNITION_TEMP = 0.5
OXIDIZER_RATIO = 1.5
HEAT_RELEASE = 0.8
SHEAR_CELLS = 2.0
OPACITY_TOTAL = 6.0
SOURCE_COEF = (-1.0, -OXIDIZER_RATIO, 1.0 + OXIDIZER_RATIO, HEAT_RELEASE)

VMEM_LIMIT = 24 * 1024 * 1024
F32 = jnp.float32
BF16 = jnp.bfloat16


def halves(value):
    upper = value.astype(BF16)
    return upper, (value - upper.astype(F32)).astype(BF16)


def pack_rows(layers, low_out, high_out):
    depth, rows, _ = layers.shape
    half = depth // 2
    for d in range(half):
        low_out[d, 0:HALO] = layers[d, 0:HALO]
        low_out[d, HALO : 2 * HALO] = layers[d + half, 0:HALO]
        high_out[d, 0:HALO] = layers[d, rows - HALO : rows]
        high_out[d, HALO : 2 * HALO] = layers[d + half, rows - HALO : rows]


def pack_columns(layers, out):
    depth, rows, columns = layers.shape
    lane = lax.broadcasted_iota(jnp.int32, (rows, columns), 1)
    packed = jnp.zeros((rows, columns), F32)
    for d in range(depth):
        turned = pltpu.roll(layers[d], (2 * HALO * d + HALO) % columns, 1)
        packed = jnp.where(lane // (2 * HALO) == d, turned, packed)
    out[...] = packed


def pack_field(source, field, depth_out, low_out, high_out, column_out):
    depth = source.shape[1]
    depth_out[field, 0:HALO] = source[field, depth - HALO : depth]
    depth_out[field, HALO : 2 * HALO] = source[field, 0:HALO]
    pack_rows(source.at[field], low_out.at[field], high_out.at[field])
    pack_columns(source.at[field], column_out.at[field])


def pack_kernel(
    state_in,
    velocity_in,
    table_in,
    depth_out,
    low_out,
    high_out,
    column_out,
    state,
    velocity,
    table,
    sems,
):
    fields, depth = state.shape[:2]
    outer = depth - HALO
    pairs = [
        (state_in, state),
        (state_in.at[:, outer:depth], depth_out.at[:, 0:HALO]),
        (state_in.at[:, 0:HALO], depth_out.at[:, HALO : 2 * HALO]),
        (velocity_in, velocity),
        (table_in, table),
    ]
    copies = [
        pltpu.make_async_copy(source, target, sems.at[i])
        for i, (source, target) in enumerate(pairs)
    ]
    for copy in copies:
        copy.start()
    copies[0].wait()
    for field in range(fields):
        pack_rows(state.at[field], low_out.at[field], high_out.at[field])
        pack_columns(state.at[field], column_out.at[field])
    for copy in copies[1:]:
        copy.wait()


def reaction(fields, rate):
    rate[...] = (
        RATE_CONST
        * fields[0]
        * fields[1]
        / (1.0 + jnp.exp(-IGNITION_SLOPE * (fields[3] - IGNITION_TEMP)))
    )


def band(cells, targets, columns):
    lane = lax.broadcasted_iota(jnp.int32, cells.shape, 1)
    apart = cells - targets
    distance = jnp.abs(apart)
    first = jnp.zeros(cells.shape, F32)
    second = jnp.zeros(cells.shape, F32)
    for k in range(HALO):
        near = distance == k + 1
        first = jnp.where(near, float(round(FIRST_COEF[k] * FIRST_SCALE)), first)
        second = jnp.where(near, float(round(SECOND_COEF[k] * SECOND_SCALE)), second)
    first = jnp.where(apart < 0, -first, first)
    return jnp.where(lane < columns, first, second).astype(BF16)


def interior_fields(fields, velocity, inner_weight, rate, padded, across, write):
    count, depth, rows, columns = fields.shape
    start = 2 * HALO
    for field in range(count):
        upper, lower = halves(fields[field].reshape(depth * rows, columns))
        across[field] = jnp.dot(
            jnp.concatenate([upper, lower], 1), inner_weight[...], preferred_element_type=F32
        )
        for d in range(depth):
            padded[field, d, start : start + rows] = fields[field, d]
    for field in range(count):
        diffusivity = DIFFUSIVITY[field]
        for d in range(depth):
            centre = fields[field, d]
            laplace = 3.0 * CENTER_COEF * centre
            along_depth = along_row = None
            for k in range(HALO):
                up = padded[field, d, start + k + 1 : start + k + 1 + rows]
                down = padded[field, d, start - k - 1 : start - k - 1 + rows]
                term = FIRST_COEF[k] * (up - down)
                along_row = term if along_row is None else along_row + term
                both = up + down
                ahead = fields[field, d + k + 1] if d + k + 1 < depth else None
                behind = fields[field, d - k - 1] if d - k - 1 >= 0 else None
                if ahead is not None and behind is not None:
                    term = FIRST_COEF[k] * (ahead - behind)
                elif ahead is not None:
                    term = FIRST_COEF[k] * ahead
                else:
                    term = -FIRST_COEF[k] * behind
                along_depth = term if along_depth is None else along_depth + term
                for cells in (ahead, behind):
                    if cells is not None:
                        both = both + cells
                laplace = laplace + SECOND_COEF[k] * both
            here = pl.ds(d * rows, rows)
            along_column = across[field, here, 0:columns]
            laplace = laplace + across[field, here, columns : 2 * columns] * (1.0 / SECOND_SCALE)
            advect = (
                velocity[0, d] * along_depth
                + velocity[1, d] * along_row
                + (velocity[2, d] * (1.0 / FIRST_SCALE)) * along_column
            )
            write(field, d, diffusivity * laplace - advect + SOURCE_COEF[field] * rate[d])


def halo_fields(part, fields, velocity, edge_velocity, halos, halo_weight, scale, write):
    depth_halo, row_above, row_below, column_below, column_above = halos
    low_velocity, high_velocity, column_velocity = edge_velocity
    depth, rows, columns = velocity.shape[1:]
    half = depth // 2
    block = 2 * HALO
    lane = lax.broadcasted_iota(jnp.int32, (rows, columns), 1)
    behind_lane = lane % block < HALO
    edges = jnp.concatenate(
        [jnp.where(behind_lane, column_below[f], column_above[f]) for f in fields], 0
    )
    upper, lower = halves(edges)
    along = jnp.dot(
        jnp.concatenate([upper, lower], 1), halo_weight[...], preferred_element_type=F32
    )
    along_columns = []
    for n, field in enumerate(fields):
        mine = along[n * rows : (n + 1) * rows]
        along_columns.append(
            mine[:, columns:] * (scale * DIFFUSIVITY[field] / SECOND_SCALE)
            - (column_velocity[...] * (scale / FIRST_SCALE)) * mine[:, :columns]
        )

    tile = (block, columns)
    sublane = lax.broadcasted_iota(jnp.int32, tile, 0)
    lane = lax.broadcasted_iota(jnp.int32, tile, 1)
    outer_lane = (lane < HALO) | (lane >= columns - HALO)
    early = sublane < HALO
    step = sublane % HALO
    below_first, below_second, above_first, above_second = [], [], [], []
    for s in range(HALO):
        first, second = FIRST_COEF[HALO - 1 - s], SECOND_COEF[HALO - 1 - s]
        below_first.append(jnp.where(step + s < HALO, -scale * first, 0.0))
        below_second.append(jnp.where(step + s < HALO, scale * second, 0.0))
        above_first.append(jnp.where(step >= s, scale * first, 0.0))
        above_second.append(jnp.where(step >= s, scale * second, 0.0))

    def edge_rows(halo, direction, first_weights, second_weights, speed, diffusivity):
        first = second = None
        for s in range(HALO):
            turned = halo if s == 0 else pltpu.roll(halo, (direction * s) % block, 0)
            one, two = first_weights[s] * turned, second_weights[s] * turned
            first = one if first is None else first + one
            second = two if second is None else second + two
        return diffusivity * second - speed * first

    for n, field in enumerate(fields):
        diffusivity = DIFFUSIVITY[field]
        for i in range(half):
            low = edge_rows(
                row_below[field, i], -1, below_first, below_second, low_velocity[i], diffusivity
            )
            high = edge_rows(
                row_above[field, i], 1, above_first, above_second, high_velocity[i], diffusivity
            )
            for d in (i, i + half):
                low_here = low if d < half else pltpu.roll(low, HALO, 0)
                high_here = pltpu.roll(high, HALO, 0) if d < half else high
                for first_row in range(0, rows, block):
                    here = slice(first_row, first_row + block)
                    value = part[field, d, here]
                    if first_row == 0:
                        value = value + jnp.where(early, low_here, 0.0)
                    if first_row + block == rows:
                        value = value + jnp.where(early, 0.0, high_here)
                    turned = pltpu.roll(
                        along_columns[n][here], (-block * d - HALO) % columns, 1
                    )
                    value = value + jnp.where(outer_lane, turned, 0.0)
                    terms = [(-1, d - k - 1 + HALO, k) for k in range(HALO) if d - k - 1 < 0]
                    terms += [
                        (1, d + k + 1 - depth + HALO, k)
                        for k in range(HALO)
                        if d + k + 1 >= depth
                    ]
                    first = second = None
                    for sign, layer, k in terms:
                        cells = depth_halo[field, layer, here]
                        one = (sign * scale * FIRST_COEF[k]) * cells
                        two = (scale * diffusivity * SECOND_COEF[k]) * cells
                        first = one if first is None else first + one
                        second = two if second is None else second + two
                    if terms:
                        value = value + (second - velocity[0, d, here] * first)
                    write(field, d, here, value)


def first_interior(
    slice_total,
    state,
    velocity,
    table,
    columns_sent,
    part,
    inner_weight,
    halo_weight,
    row_weight,
    column_weight,
    packed_table,
    low_velocity,
    high_velocity,
    column_velocity,
    rate,
    padded,
    across,
):
    del columns_sent
    _, depth, rows, columns = state.shape
    shape = inner_weight.shape
    index = lax.broadcasted_iota(jnp.int32, shape, 0) % columns
    target = lax.broadcasted_iota(jnp.int32, shape, 1) % columns
    inner_weight[...] = band(index, target, columns)
    edge, target_edge = index % (2 * HALO), target % (2 * HALO)
    weight = band(
        jnp.where(edge < HALO, edge, edge + columns) - HALO,
        jnp.where(target_edge < HALO, target_edge + columns, target_edge) - HALO,
        columns,
    )
    same_layer = index // (2 * HALO) == target // (2 * HALO)
    halo_weight[...] = jnp.where(same_layer, weight, jnp.zeros_like(weight))
    pack_rows(velocity.at[1], low_velocity, high_velocity)
    pack_columns(velocity.at[2], column_velocity)
    shape = column_weight.shape
    cell = (lax.broadcasted_iota(jnp.int32, shape, 0) % columns).astype(F32)
    pixel = (lax.broadcasted_iota(jnp.int32, shape, 1) % PIX_C).astype(F32)
    column_weight[...] = tent(pixel, cell, 0.0, columns, PIX_C).astype(BF16)
    half = depth // 2
    place = lax.axis_index("depth") * depth
    shape = (PIX_R, row_weight.shape[2])
    pixel = lax.broadcasted_iota(jnp.int32, shape, 0).astype(F32)
    lane = lax.broadcasted_iota(jnp.int32, shape, 1)
    cell = (lane % rows).astype(F32)
    later = (lane // rows % 2) * half
    for i in range(half):
        level = (place + i + later).astype(F32)
        shift = SHEAR_CELLS * ((level + 0.5) / slice_total - 0.5)
        row_weight[i] = tent(pixel, cell, shift, rows, PIX_R).astype(BF16)
    levels = table.shape[1]
    packed = table[0:1] + table[1:2] * 256 + table[2:3] * 65536 + table[3:4] * 16777216
    packed_table[0:1] = packed
    packed_table[1:2] = jnp.concatenate([packed[:, 1:], packed[:, levels - 1 :]], 1)
    padded[...] = jnp.zeros_like(padded)
    reaction(state, rate)

    def write(field, d, value):
        part[field, d] = state[field, d] + TIME_STEP * value

    interior_fields(state, velocity, inner_weight, rate, padded, across, write)


def first_halo(
    part,
    velocity,
    low_velocity,
    high_velocity,
    column_velocity,
    depth_halo,
    row_above,
    row_below,
    column_below,
    column_above,
    halo_weight,
    middle,
    depth_out,
    low_out,
    high_out,
    column_out,
):
    halos = (depth_halo, row_above, row_below, column_below, column_above)
    edge_velocity = (low_velocity, high_velocity, column_velocity)

    def write(field, d, here, value):
        middle[field, d, here] = value

    fields = range(part.shape[0])
    halo_fields(part, fields, velocity, edge_velocity, halos, halo_weight, TIME_STEP, write)
    for field in fields:
        pack_field(middle, field, depth_out, low_out, high_out, column_out)


def second_interior(
    middle, state, velocity, inner_weight, columns_sent, part, rate, padded, across
):
    del columns_sent
    padded[...] = jnp.zeros_like(padded)
    reaction(middle, rate)

    def write(field, d, value):
        part[field, d] = 0.5 * (state[field, d] + middle[field, d]) + (0.5 * TIME_STEP) * value

    interior_fields(middle, velocity, inner_weight, rate, padded, across, write)


def tent(pixel, cell, shift, cells, pixels):
    stride = cells / pixels
    reach = max(1.0, stride)
    at = jnp.clip((pixel + 0.5) * stride - 0.5 + shift, 0.0, cells - 1.0)
    return jnp.maximum(0.0, 1.0 - jnp.abs(at - cell) / reach) / reach


def sample_slices(temperature, scale, column_weight, row_weight, samples):
    depth, rows, columns = temperature.shape
    half = depth // 2
    upper, lower = halves(temperature[...].reshape(depth * rows, columns) * scale)
    wide = jnp.dot(
        jnp.concatenate([upper, lower], 1), column_weight[...], preferred_element_type=F32
    )
    lane = lax.broadcasted_iota(jnp.int32, (rows, 2 * PIX_C), 1)
    for i in range(half):
        left = jnp.where(lane < PIX_C, wide[i * rows : (i + 1) * rows], 0.0)
        right = jnp.where(
            lane < PIX_C, 0.0, wide[(i + half) * rows : (i + half + 1) * rows]
        )
        both_upper, both_lower = halves(jnp.concatenate([left, right], 0))
        samples[i] = jnp.dot(
            row_weight[i],
            jnp.concatenate([both_upper, both_lower], 0),
            preferred_element_type=F32,
        )


def look_up(tables, index, shape):
    lanes = tables[0].shape[1]
    inside = index & (lanes - 1)
    result = None
    for part, table in enumerate(tables):
        found = jnp.take_along_axis(
            jnp.broadcast_to(table, shape), inside, axis=1, mode="promise_in_bounds"
        )
        result = found if part == 0 else jnp.where(index >= part * lanes, found, result)
    return result


def march(samples, table, flag, slice_total, share):
    half, pixel_rows, lanes = samples.shape
    levels = table.shape[1]
    below_tables = [table[0:1, i : i + lanes] for i in range(0, levels, lanes)]
    above_tables = [table[1:2, i : i + lanes] for i in range(0, levels, lanes)]
    shape = (pixel_rows // 2, lanes)
    lane = lax.broadcasted_iota(jnp.int32, shape, 1)
    in_front = (lane < PIX_C) == (flag == 0)
    parts = []
    for part in range(2):
        rows_here = pl.ds(part * shape[0], shape[0])

        def advance(position, running):
            chosen = jnp.where(flag == 0, half - 1 - position, position)
            level = jnp.clip(samples[chosen, rows_here], 0.0, levels - 1.0)
            lower = level.astype(jnp.int32)
            fraction = level - lower.astype(F32)
            below = look_up(below_tables, lower, shape)
            above = look_up(above_tables, lower, shape)
            low_alpha = lax.shift_right_logical(below, 24).astype(F32)
            high_alpha = lax.shift_right_logical(above, 24).astype(F32)
            alpha = (low_alpha + fraction * (high_alpha - low_alpha)) * (
                OPACITY_TOTAL / slice_total / 255.0
            )
            through = 1.0 - alpha
            high_share = alpha * fraction
            low_share = alpha - high_share
            result = []
            for channel in range(3):
                low = (below & (255 << 8 * channel)).astype(F32)
                high = (above & (255 << 8 * channel)).astype(F32)
                result.append(
                    through * running[channel] + (low_share * low + high_share * high)
                )
            return tuple(result + [alpha + through * running[3]])

        zero = jnp.zeros(shape, F32)
        running = lax.fori_loop(0, half, advance, (zero, zero, zero, zero), unroll=True)
        parts.append(
            [running[c] * (1.0 / 255.0 / 256.0**c) for c in range(3)] + [running[3]]
        )
    for channel in range(4):
        merged = []
        for part in range(2):
            own, own_alpha = parts[part][channel], parts[part][3]
            other, other_alpha = pltpu.roll(own, PIX_C, 1), pltpu.roll(own_alpha, PIX_C, 1)
            merged.append(
                jnp.where(
                    in_front, own + (1.0 - own_alpha) * other, other + (1.0 - other_alpha) * own
                )
            )
        share[channel] = jnp.where(lane < PIX_C, merged[0], merged[1])


def temperature_halo(
    slice_total,
    order,
    part,
    velocity,
    low_velocity,
    high_velocity,
    column_velocity,
    depth_halo,
    row_above,
    row_below,
    column_below,
    column_above,
    halo_weight,
    column_weight,
    row_weight,
    table,
    temperature,
    share,
    toward,
    samples,
):
    halos = (depth_halo, row_above, row_below, column_below, column_above)
    edge_velocity = (low_velocity, high_velocity, column_velocity)

    def write(field, d, here, value):
        temperature[d, here] = value

    halo_fields(part, [3], velocity, edge_velocity, halos, halo_weight, 0.5 * TIME_STEP, write)
    sample_slices(temperature, table.shape[1] - 1.0, column_weight, row_weight, samples)
    toward[...] = jnp.full(toward.shape, order[0, 0], jnp.int32)
    march(samples, table, order[0, 0], slice_total, share)


def fractions_halo(
    part,
    temperature,
    velocity,
    low_velocity,
    high_velocity,
    column_velocity,
    depth_halo,
    row_above,
    row_below,
    column_below,
    column_above,
    halo_weight,
    share,
    new_state,
):
    del share
    halos = (depth_halo, row_above, row_below, column_below, column_above)
    edge_velocity = (low_velocity, high_velocity, column_velocity)

    def write(field, d, here, value):
        new_state[field, d, here] = value

    halo_fields(
        part, range(3), velocity, edge_velocity, halos, halo_weight, 0.5 * TIME_STEP, write
    )
    new_state[3] = temperature[...]


def merge_kernel(bit, last, toward, own, received, out):
    shape = own.shape[1:]
    mine = lax.axis_index("depth") // 2**bit % 2
    front = jnp.broadcast_to(toward[0:1] == mine, shape)
    own_alpha, received_alpha = own[3], received[3]
    for channel in range(4):
        one, two = own[channel], received[channel]
        front_value = one + (1.0 - own_alpha) * two
        back_value = two + (1.0 - received_alpha) * one
        value = jnp.where(front, front_value, back_value)
        if last:
            out[channel, 0 : shape[0]] = value[:, 0:PIX_C]
            out[channel, shape[0] : 2 * shape[0]] = pltpu.roll(value, PIX_C, 1)[:, 0:PIX_C]
        else:
            out[channel] = value


def shift(value, axis, step):
    count = lax.axis_size(axis)
    return lax.ppermute(value, axis, [(i, (i + step) % count) for i in range(count)])


def exchange(depth_faces, low_rows, high_rows, columns):
    if lax.axis_size("depth") == 2:
        depth_halo = shift(depth_faces, "depth", 1)
    else:
        depth_halo = jnp.concatenate(
            [
                shift(depth_faces[:, :HALO], "depth", 1),
                shift(depth_faces[:, HALO:], "depth", -1),
            ],
            1,
        )
    row_below = shift(high_rows, "row", 1)
    row_above = shift(low_rows, "row", -1)
    column_below = shift(columns, "col", 1)
    column_above = shift(columns, "col", -1)
    return depth_halo, row_above, row_below, column_below, column_above


def call(kernel, outs, scratch, specs, *args):
    vmem = pl.BlockSpec(memory_space=pltpu.VMEM)
    return pl.pallas_call(
        kernel,
        out_shape=outs,
        in_specs=specs + [vmem] * (len(args) - len(specs)),
        out_specs=jax.tree.map(lambda _: vmem, outs),
        scratch_shapes=scratch,
        compiler_params=pltpu.CompilerParams(vmem_limit_bytes=VMEM_LIMIT),
    )(*args)


def in_hbm(value):
    return pltpu.with_memory_space_constraint(value, pltpu.HBM)


def local(state, velocity, view_order, tf_table):
    fields, depth, rows, columns = state.shape
    depth_count = lax.axis_size("depth")

    def array(*shape, dtype=F32):
        return jax.ShapeDtypeStruct(shape, dtype)

    whole = array(*state.shape)
    faces = (
        array(fields, 2 * HALO, rows, columns),
        array(fields, depth // 2, 2 * HALO, columns),
        array(fields, depth // 2, 2 * HALO, columns),
        array(fields, rows, columns),
    )
    inner_work = [
        pltpu.VMEM((depth, rows, columns), F32),
        pltpu.VMEM((fields, depth, rows + 4 * HALO, columns), F32),
        pltpu.VMEM((fields, depth * rows, 2 * columns), F32),
    ]
    edge_rows = array(depth // 2, 2 * HALO, columns)
    slice_total = depth * depth_count

    hbm = pl.BlockSpec(memory_space=pltpu.HBM)
    *sent, state, velocity, table = call(
        pack_kernel,
        faces + (whole, array(*velocity.shape), array(*tf_table.shape, dtype=jnp.int32)),
        [pltpu.SemaphoreType.DMA((5,))],
        [hbm, hbm, hbm],
        in_hbm(state),
        in_hbm(velocity),
        in_hbm(tf_table),
    )
    halos = exchange(*sent)
    part, inner_weight, halo_weight, row_weight, column_weight, table, *edge_velocity = call(
        functools.partial(first_interior, slice_total),
        (
            whole,
            array(2 * columns, 2 * columns, dtype=BF16),
            array(2 * columns, 2 * columns, dtype=BF16),
            array(depth // 2, PIX_R, 4 * rows, dtype=BF16),
            array(2 * columns, 2 * PIX_C, dtype=BF16),
            array(2, tf_table.shape[1], dtype=jnp.int32),
            edge_rows,
            edge_rows,
            array(rows, columns),
        ),
        inner_work,
        [],
        state,
        velocity,
        table,
        sent[3],
    )
    middle, *sent = call(
        first_halo,
        (whole,) + faces,
        [],
        [],
        part,
        velocity,
        *edge_velocity,
        *halos,
        halo_weight,
    )
    halos = exchange(*sent)
    part = call(
        second_interior,
        whole,
        inner_work,
        [],
        middle,
        state,
        velocity,
        inner_weight,
        sent[3],
    )
    temperature, share, toward = call(
        functools.partial(temperature_halo, slice_total),
        (
            array(depth, rows, columns),
            array(4, PIX_R // 2, 2 * PIX_C),
            array(8, 2 * PIX_C, dtype=jnp.int32),
        ),
        [pltpu.VMEM((depth // 2, PIX_R, 2 * PIX_C), F32)],
        [pl.BlockSpec(memory_space=pltpu.SMEM)],
        view_order,
        part,
        velocity,
        *edge_velocity,
        *halos,
        halo_weight,
        column_weight,
        row_weight,
        table,
    )
    new_state = call(
        fractions_halo,
        whole,
        [],
        [],
        part,
        temperature,
        velocity,
        *edge_velocity,
        *halos,
        halo_weight,
        share,
    )
    bits = depth_count.bit_length() - 1
    for bit in range(bits):
        pairs = [(i, i ^ 2**bit) for i in range(depth_count)]
        received = lax.ppermute(share, "depth", pairs)
        last = bit == bits - 1
        share = call(
            functools.partial(merge_kernel, bit, last),
            array(4, PIX_R, PIX_C) if last else array(*share.shape),
            [],
            [],
            toward,
            share,
            received,
        )
    return new_state, share


def solution(mesh):
    in_specs = (
        P(None, "depth", "row", "col"),
        P(None, "depth", "row", "col"),
        P("row", "col"),
        P(),
    )
    out_specs = (P(None, "depth", "row", "col"), P(None, "row", "col"))
    return jax.shard_map(local, mesh=mesh, in_specs=in_specs, out_specs=out_specs, check_vma=False)
```
